256 devices in a mesh: wide: 32 (over x, y, core), narrow: 8 (over z).
Axes of the slice: x: 4, y: 4, z: 8, core: 2. Of those that a mesh axis runs over, the one named last changes fastest.
Arguments:
- embeddings: bfloat16 [524288, 1536], P(('wide', 'narrow')), may hold values from -6 to 6
- point_counts: int32 [524288], P(('wide', 'narrow')), may hold values from 1 to 64
- owner_ids: int32 [524288, 1], P(('wide', 'narrow')), may hold values from 0 to 255; in each aligned block of 2048 rows (0 to 2047, 2048 to 4095, ...) at most 16 rows name the same one
- owner_slots: int32 [524288, 1], P(('wide', 'narrow')), may hold values from 0 to 255
- reseed_slots: int32 [256, 2], P(('wide', 'narrow')), may hold values from 0 to 255, as said below
- donor_ids: int32 [256, 2], P(('wide', 'narrow')), may hold values from 0 to 524287
- parents_two: int32 [65536], P(('wide', 'narrow')), may hold values from 0 to 1023
- parents_three: int32 [1024], P('narrow'), may hold values from 0 to 255
Outputs:
- level_two: float32 [65536, 1536], P(('wide', 'narrow'))
- level_three: float32 [1024, 1536], P('narrow')
- level_four: float32 [256, 1536], replicated
The draws below stay inside these ranges and needn't reach their ends.
Inputs may be any that keep to these rules, and one draw needn't show every extreme that they name: `owner_ids`: among the level-1 centroids of one device at most 16 have their parent on one owner, and some owner has exactly 16. `reseed_slots`: the entries of one device's row are different.
All inputs are finite; a program needn't handle non-finite values.
Results may differ from the reference program's by a relative error of at most 0.0003.
Values may be sent and summed in bfloat16 or wider, within the bound.
A program may use at most 128 MiB of HBM per device.

```python
import math
import jax
import jax.numpy as jnp
import numpy as np
from jax import lax

D = 1536
R1 = 2048
L4 = 256
RES = 2
L2_DEV = 256
CAP = 16
TOTAL1 = 524288
TOTAL2 = 65536
TOTAL3 = 1024
N_WIDE = 32
N_NARROW = 8


def draw_embeddings(key, part):
    key = jax.random.fold_in(key, 11)
    key_mean, key_noise = jax.random.split(key, 2)
    common = jax.random.normal(key_mean, (D,), jnp.float32)
    values = 0.6 * common[None, :] + jax.random.normal(key_noise, (TOTAL1, D), jnp.float32)
    return jnp.clip(values, -6.0, 6.0).astype(jnp.bfloat16)


def draw_reseed_slots(key, part):
    key = jax.random.fold_in(key, 12)
    stride = L2_DEV // RES
    offsets = jax.random.randint(key, (N_WIDE * N_NARROW, RES), 0, stride, jnp.int32)
    return offsets + jnp.arange(RES, dtype=jnp.int32)[None, :] * stride


def touch_ends(result, stream_key, low, high):
    longest = result.shape.index(max(result.shape))
    spots = []
    for shift in (0, 1):
        where = [jax.random.randint(jax.random.fold_in(stream_key, axis), (), 0, length) for axis, length in enumerate(result.shape)]
        where[longest] = (where[longest] + shift) % result.shape[longest]
        spots.append(tuple(where))
    return result.at[spots[0]].set(low).at[spots[1]].set(high)


def shared_out(key, own, number, rows, number_of, top, bound, lean):
    order = jax.random.permutation(key, number_of)
    crowded, usual = shares(number_of, rows * top, bound, lean, True), shares(number_of, rows * top, bound, lean, False)
    places = jnp.arange(number_of)

    def named(sizes, offset_by):
        used = int((sizes > 0).sum())
        fixed = max(1, used // 4)
        shifted = fixed + (places - fixed + offset_by * (used - fixed)) % max(1, number_of - fixed)
        return jnp.zeros((number_of,), jnp.int32).at[order[jnp.where(places < fixed, places, shifted)]].set(jnp.asarray(sizes, jnp.int32))

    sizes = jnp.where(number % 4 == 0, named(crowded, number // 4), named(usual, number - number // 4 - 1))
    mixed = jax.random.permutation(jax.random.fold_in(own, 3), number_of)
    source_of, taker = mixed[0:number_of // 2 * 2:2], mixed[1:number_of // 2 * 2:2]
    margin = jnp.minimum(sizes[source_of] - 1, bound - sizes[taker]) // 2
    margin = jnp.where((source_of == order[0]) | (taker == order[0]) | (sizes[taker] == 0), 0, jnp.maximum(margin, 0))
    shifted = jax.random.randint(jax.random.fold_in(own, 4), (number_of // 2,), 0, 1 << 20) % (margin + 1)
    sizes = sizes.at[source_of].add(-shifted).at[taker].add(shifted)
    labels = jnp.searchsorted(jnp.cumsum(sizes), jnp.arange(rows * top), side="right").astype(jnp.int32)
    table = labels.reshape(top, rows).T
    table = table[jax.random.permutation(jax.random.fold_in(own, 1), rows)]
    offset_by = jax.random.randint(jax.random.fold_in(own, 2), (rows, 1), 0, top)
    return jnp.take_along_axis(table, (jnp.arange(top)[None, :] + offset_by) % top, axis=1)


def shares(number_of, total, most, skew, full):
    weights = [(1 << 20) // math.isqrt(rank ** skew) + 1 for rank in range(1, number_of + 1)]
    largest = most if full else min(most, max(-(-total // number_of), total * weights[0] // sum(weights)))
    least = 1 if total - largest >= number_of - 1 else 0
    holding, surplus = [largest] + [least] * (number_of - 1), total - largest - least * (number_of - 1)
    while surplus > 0:
        candidates = [i for i in range(1, number_of) if holding[i] < largest] or [i for i in range(1, number_of) if holding[i] < most]
        mass, remaining = sum([weights[i] for i in candidates]), surplus
        for i in candidates:
            more = min(most - holding[i], max(1, remaining * weights[i] // mass), surplus)
            holding[i] = holding[i] + more
            surplus = surplus - more
    return np.array(holding)


def setup_inputs(seed: int = 0) -> dict:
    keys = jax.random.split(jax.random.key(seed), 9)
    embeddings = draw_embeddings(jax.random.fold_in(keys[8], 71), 0)
    point_counts = touch_ends(jax.random.randint(keys[1], (TOTAL1,), 1, 65), jax.random.fold_in(keys[1], 1), 1, 64).astype(jnp.int32)
    owner_ids_keys = jax.random.split(jax.random.fold_in(keys[2], 1), TOTAL1 // R1)
    owner_ids_turns = jax.random.permutation(jax.random.fold_in(keys[2], 3), TOTAL1 // R1)
    owner_ids = jax.vmap(lambda own, number: shared_out(jax.random.fold_in(keys[2], 2), own, number, R1, N_WIDE * N_NARROW, 1, CAP, 2))(owner_ids_keys, owner_ids_turns).reshape((TOTAL1, 1))
    owner_slots = touch_ends(jax.random.randint(keys[3], (TOTAL1, 1), 0, L2_DEV), jax.random.fold_in(keys[3], 1), 0, L2_DEV - 1).astype(jnp.int32)
    reseed_slots = draw_reseed_slots(jax.random.fold_in(keys[8], 71), 0)
    donor_ids = touch_ends(jax.random.randint(keys[5], (N_WIDE * N_NARROW, RES), 0, TOTAL1), jax.random.fold_in(keys[5], 1), 0, TOTAL1 - 1).astype(jnp.int32)
    parents_two = touch_ends(jax.random.randint(keys[6], (TOTAL2,), 0, TOTAL3), jax.random.fold_in(keys[6], 1), 0, TOTAL3 - 1).astype(jnp.int32)
    parents_three = touch_ends(jax.random.randint(keys[7], (TOTAL3,), 0, L4), jax.random.fold_in(keys[7], 1), 0, L4 - 1).astype(jnp.int32)
    return dict(embeddings=embeddings, point_counts=point_counts, owner_ids=owner_ids, owner_slots=owner_slots, reseed_slots=reseed_slots, donor_ids=donor_ids, parents_two=parents_two, parents_three=parents_three)


def reference(embeddings, point_counts, owner_ids, owner_slots, reseed_slots, donor_ids, parents_two, parents_three):
    device_total = N_WIDE * N_NARROW
    parent_one = owner_ids[:, 0] * L2_DEV + owner_slots[:, 0]
    weights_one = point_counts.astype(jnp.float32)

    def accumulate(running, block_index):
        begin_row = block_index * R1
        block_values = lax.dynamic_slice_in_dim(embeddings, begin_row, R1).astype(jnp.float32)
        block_weights = lax.dynamic_slice_in_dim(weights_one, begin_row, R1)
        block_parents = lax.dynamic_slice_in_dim(parent_one, begin_row, R1)
        return running.at[block_parents].add(block_values * block_weights[:, None]), None

    sums_two, unused = lax.scan(accumulate, jnp.zeros((TOTAL2, D), jnp.float32), jnp.arange(device_total, dtype=jnp.int32))
    weight_two = jax.ops.segment_sum(weights_one, parent_one, num_segments=TOTAL2)
    level_two = sums_two / jnp.maximum(weight_two, 1.0)[:, None]
    reseed_rows = (jnp.arange(device_total, dtype=jnp.int32)[:, None] * L2_DEV + reseed_slots).reshape(-1)
    level_two = level_two.at[reseed_rows].set(embeddings[donor_ids.reshape(-1)].astype(jnp.float32))
    sums_three = jax.ops.segment_sum(weight_two[:, None] * level_two, parents_two, num_segments=TOTAL3)
    weight_three = jax.ops.segment_sum(weight_two, parents_two, num_segments=TOTAL3)
    level_three = sums_three / jnp.maximum(weight_three, 1.0)[:, None]
    sums_four = jax.ops.segment_sum(weight_three[:, None] * level_three, parents_three, num_segments=L4)
    weight_four = jax.ops.segment_sum(weight_three, parents_three, num_segments=L4)
    level_four = sums_four / jnp.maximum(weight_four, 1.0)[:, None]
    return (level_two, level_three, level_four)
```

```python
import functools

import jax
import jax.numpy as jnp
from jax import lax
from jax.experimental import pallas as pl
from jax.experimental.pallas import tpu as pltpu
from jax.sharding import PartitionSpec as P

L4 = 256
CAP = 16
NX, NY, NC, NZ = 4, 4, 2, 8
NW = NX * NY * NC
MESH = pl.DeviceIdType.MESH
SEND_BUFFERS = 3

XY_ORDER = [
    (1, 0), (0, 1), (3, 0), (0, 3), (2, 2), (1, 1), (3, 3), (1, 3),
    (3, 1), (2, 0), (0, 2), (2, 1), (1, 2), (2, 3), (3, 2),
]
WIDE_ORDER = [(dx, dy, dc) for dc in range(NC) for dx, dy in XY_ORDER] + [(0, 0, 1)]


def nt_dot(a, b):
    return lax.dot_general(
        a, b, (((1,), (1,)), ((), ())), preferred_element_type=jnp.float32
    )


def iota(shape, axis):
    return lax.broadcasted_iota(jnp.int32, shape, axis)


def exchange_kernel(
    emb, own, slot, cnt,
    out, weight_out,
    sbuf, rbuf, onehot, pos, lab_send, lab_recv, lab_t, ring_f, ring_b, w_send, w_recv,
    s_sem, r_sem, lab_sems, f_send, f_recv, b_send, b_recv, w_sems,
):
    rows, width = emb.shape
    half = width // 2
    w = lax.axis_index("wide")
    z = lax.axis_index("narrow")
    x, y, c = w // 8, (w // 2) % 4, w % 2

    def wide_peer(d):
        return (((x + d[0]) % NX) * 8 + ((y + d[1]) % NY) * 2 + (c + d[2]) % NC, z)

    def z_peer(k):
        return (w, (z + k) % NZ)

    barrier = pltpu.get_barrier_semaphore()
    for d in WIDE_ORDER:
        pl.semaphore_signal(barrier, inc=1, device_id=wide_peer(d), device_id_type=MESH)
    for k in range(1, NZ):
        pl.semaphore_signal(barrier, inc=1, device_id=z_peer(k), device_id_type=MESH)

    owner = own[...]
    target = owner // NZ
    rel = (
        ((target // 8 - x) & 3) * 8 + (((target // 2) - y) & 3) * 2 + ((target - c) & 1)
    )
    step = 256
    upper = (iota((step, step), 0) < iota((step, step), 1)).astype(jnp.bfloat16)
    carry = jnp.zeros((step, 1), jnp.float32)
    for b in range(rows // step):
        cols = slice(b * step, (b + 1) * step)
        hit = iota((step, step), 0) == owner[:, cols]
        mark = hit.astype(jnp.bfloat16)
        earlier = jnp.dot(mark, upper, preferred_element_type=jnp.float32) + carry
        mark32 = hit.astype(jnp.float32)
        rank = jnp.sum(earlier * mark32, axis=0, keepdims=True)
        carry = carry + jnp.sum(mark32, axis=1, keepdims=True)
        pos[0:1, cols] = rel[:, cols] * CAP + rank.astype(jnp.int32)
    pos[1:2, :] = owner % NZ

    places = NW * CAP
    tile = 256

    def fill_onehot(where_row):
        for i in range(places // tile):
            ids = iota((tile, rows), 0) + i * tile
            onehot[i * tile : (i + 1) * tile, :] = (ids == where_row).astype(jnp.bfloat16)

    fill_onehot(pos[0:1, :])
    lane = iota((128, rows), 0)
    z_of = pos[1:2, :]
    labels = jnp.where(
        lane == 2 * z_of, slot[...], jnp.where(lane == 2 * z_of + 1, cnt[...], 0)
    ).astype(jnp.float32).astype(jnp.bfloat16)
    lab_send[...] = nt_dot(onehot[...], labels).astype(jnp.bfloat16)
    lab_recv[0:CAP, :] = lab_send[0:CAP, :]

    pl.semaphore_wait(barrier, NW - 1 + NZ - 1)

    def send_wide(src, dst, sem_s, sem_r):
        for d in WIDE_ORDER:
            k = d[0] * 8 + d[1] * 2 + d[2]
            at = pl.ds(k * CAP, CAP)
            pltpu.make_async_remote_copy(
                src_ref=src.at[at], dst_ref=dst.at[at], send_sem=sem_s, recv_sem=sem_r,
                device_id=wide_peer(d), device_id_type=MESH,
            ).start()

    def all_wide(src, dst, sem_s, sem_r):
        at = pl.ds(CAP, places - CAP)
        return pltpu.make_async_remote_copy(
            src_ref=src.at[at], dst_ref=dst.at[at], send_sem=sem_s, recv_sem=sem_r,
            device_id=wide_peer((0, 0, 1)), device_id_type=MESH,
        )

    send_wide(lab_send, lab_recv, lab_sems.at[0], lab_sems.at[1])

    def block_f(t):
        return (z + 2 * NZ - 1 - t) % NZ

    def block_b(t):
        return (z + 1 + t) % NZ

    def pack_and_send(t):
        b = lax.rem(t, SEND_BUFFERS)

        @pl.when(t >= SEND_BUFFERS)
        def _():
            all_wide(sbuf.at[b], rbuf.at[t], s_sem.at[b], r_sem.at[t]).wait_send()

        for h, blk in enumerate((block_f(t), block_b(t))):
            fill_onehot(jnp.where(pos[1:2, :] == blk, pos[0:1, :], -1))

            def column(n, _, h=h):
                at = pl.ds(pl.multiple_of(h * half + n * tile, tile), tile)
                sbuf[b, :, at] = jnp.dot(
                    onehot[...], emb[:, at], preferred_element_type=jnp.float32
                ).astype(jnp.bfloat16)
                return 0

            lax.fori_loop(0, half // tile, column, 0)
        rbuf[t, 0:CAP, :] = sbuf[b, 0:CAP, :]
        send_wide(sbuf.at[b], rbuf.at[t], s_sem.at[b], r_sem.at[t])

    pack_and_send(0)

    all_wide(lab_send, lab_recv, lab_sems.at[0], lab_sems.at[1]).wait()
    eye = (iota((16, 128), 0) == iota((16, 128), 1)).astype(jnp.bfloat16)
    lab_t[...] = nt_dot(eye, lab_recv[...])
    clusters = out.shape[0]

    def matched(blk):
        ids = iota((clusters, places), 0).astype(jnp.float32)
        return ids == lab_t[pl.ds(2 * blk, 1), :], lab_t[pl.ds(2 * blk + 1, 1), :]

    def weigh(k, _):
        hit, counts = matched((z + k) % NZ)
        counts = jnp.broadcast_to(counts, (8, places)).astype(jnp.bfloat16)
        w_send[k] = nt_dot(counts, hit.astype(jnp.float32).astype(jnp.bfloat16))
        return 0

    lax.fori_loop(0, NZ, weigh, 0)

    def weight_copy(src, dst, k):
        return pltpu.make_async_remote_copy(
            src_ref=src, dst_ref=dst, send_sem=w_sems.at[0], recv_sem=w_sems.at[1],
            device_id=z_peer(k), device_id_type=MESH,
        )

    for k in range(1, NZ):
        weight_copy(w_send.at[k], w_recv.at[k], k).start()

    def ring_copy(ring, t, sems, k):
        return pltpu.make_async_remote_copy(
            src_ref=ring.at[t], dst_ref=ring.at[t + 1],
            send_sem=sems[0].at[t], recv_sem=sems[1].at[t + 1],
            device_id=z_peer(k), device_id_type=MESH,
        )

    rings = (
        (ring_f, (f_send, f_recv), 1, block_f),
        (ring_b, (b_send, b_recv), NZ - 1, block_b),
    )

    def reduce_stage(t):
        all_wide(sbuf.at[0], rbuf.at[t], s_sem.at[0], r_sem.at[t]).wait_recv()
        for h, (ring, sems, k, block) in enumerate(rings):
            hit, counts = matched(block(t))
            assign = jnp.where(hit, counts, 0.0).astype(jnp.bfloat16)

            @pl.when(t > 0)
            def _(ring=ring, sems=sems, k=k):
                ring_copy(ring, t - 1, sems, k).wait_recv()

            for n in range(half // tile):
                at = slice(n * tile, (n + 1) * tile)
                part = jnp.dot(
                    assign,
                    rbuf[t, :, h * half + n * tile : h * half + (n + 1) * tile],
                    preferred_element_type=jnp.float32,
                )

                @pl.when(t == 0)
                def _(ring=ring, at=at, part=part):
                    ring[t, :, at] = part

                @pl.when(t > 0)
                def _(ring=ring, at=at, part=part):
                    ring[t, :, at] += part

            @pl.when(t < NZ - 1)
            def _(ring=ring, sems=sems, k=k):
                ring_copy(ring, t, sems, k).start()

    def stage(t, _):
        @pl.when(t < NZ - 1)
        def _():
            pack_and_send(t + 1)

        reduce_stage(t)
        return 0

    lax.fori_loop(0, NZ, stage, 0)

    others = pl.ds(1, NZ - 1)
    weight_copy(w_send.at[others], w_recv.at[others], 1).wait()
    total = w_send[0]
    for k in range(1, NZ):
        total = total + w_recv[k]
    weight_out[...] = total
    diagonal = iota((clusters, clusters), 0) == iota((clusters, clusters), 1)
    column_w = jnp.sum(jnp.where(diagonal, total[0:1, :], 0.0), axis=1, keepdims=True)
    column_w = jnp.maximum(column_w, 1.0)
    for h, (ring, sems, k, block) in enumerate(rings):
        for n in range(half // tile):
            at = slice(n * tile, (n + 1) * tile)
            out[:, h * half + n * tile : h * half + (n + 1) * tile] = (
                ring[NZ - 1, :, at] / column_w
            )

    for b in range(SEND_BUFFERS):
        all_wide(sbuf.at[b], rbuf.at[0], s_sem.at[b], r_sem.at[0]).wait_send()
    for ring, sems, k, block in rings:
        def drain(t, _, ring=ring, sems=sems, k=k):
            ring_copy(ring, t, sems, k).wait_send()
            return 0

        lax.fori_loop(0, NZ - 1, drain, 0)


def exchange(embeddings, owner_ids, owner_slots, point_counts, clusters):
    rows, width = embeddings.shape
    places = NW * CAP
    vmem = pl.BlockSpec(memory_space=pltpu.VMEM)
    dma = pltpu.SemaphoreType.DMA
    return pl.pallas_call(
        exchange_kernel,
        out_shape=(
            jax.ShapeDtypeStruct((clusters, width), jnp.float32),
            jax.ShapeDtypeStruct((8, clusters), jnp.float32),
        ),
        in_specs=[vmem] * 4,
        out_specs=(vmem, vmem),
        scratch_shapes=[
            pltpu.VMEM((SEND_BUFFERS, places, width), jnp.bfloat16),
            pltpu.VMEM((NZ, places, width), jnp.bfloat16),
            pltpu.VMEM((places, rows), jnp.bfloat16),
            pltpu.VMEM((8, rows), jnp.int32),
            pltpu.VMEM((places, 128), jnp.bfloat16),
            pltpu.VMEM((places, 128), jnp.bfloat16),
            pltpu.VMEM((16, places), jnp.float32),
            pltpu.VMEM((NZ, clusters, width // 2), jnp.float32),
            pltpu.VMEM((NZ, clusters, width // 2), jnp.float32),
            pltpu.VMEM((NZ, 8, clusters), jnp.float32),
            pltpu.VMEM((NZ, 8, clusters), jnp.float32),
            dma((SEND_BUFFERS,)),
            dma((NZ,)),
            dma((2,)),
            dma((NZ,)),
            dma((NZ,)),
            dma((NZ,)),
            dma((NZ,)),
            dma((2,)),
        ],
        compiler_params=pltpu.CompilerParams(
            collective_id=0, has_side_effects=True, vmem_limit_bytes=60 * 2**20
        ),
    )(
        embeddings,
        owner_ids.reshape(1, rows),
        owner_slots.reshape(1, rows),
        point_counts.reshape(1, rows),
    )


def per_device(
    embeddings,
    point_counts,
    owner_ids,
    owner_slots,
    reseed_slots,
    donor_ids,
    parents_two,
    parents_three,
):
    narrow_count = lax.axis_size("narrow")
    rows_local, feature_width = embeddings.shape
    clusters = parents_two.shape[0]
    requests = lax.all_gather(donor_ids[0], ("wide", "narrow"), axis=0, tiled=True)
    first_row = lax.axis_index(("wide", "narrow")) * rows_local
    local_row = requests - first_row
    inside = (local_row >= 0) & (local_row < rows_local)
    picked = embeddings[jnp.clip(local_row, 0, rows_local - 1)].astype(jnp.float32)
    donor_rows = lax.psum_scatter(
        jnp.where(inside[:, None], picked, 0.0), ("wide", "narrow"), scatter_dimension=0, tiled=True
    )
    centre_two, weight_rows = exchange(
        embeddings, owner_ids, owner_slots, point_counts, clusters
    )
    weight_two = weight_rows[0]
    centre_two = centre_two.at[reseed_slots[0]].set(donor_rows)
    per_owner = parents_three.shape[0]
    total_three = per_owner * narrow_count
    rows_three = jnp.arange(total_three, dtype=jnp.int32)
    assign_three = jnp.where(parents_two[None, :] == rows_three[:, None], weight_two[None, :], 0.0)
    partial_value = jnp.dot(
        assign_three,
        centre_two,
        precision=lax.Precision.HIGHEST,
        preferred_element_type=jnp.float32,
    )
    masses = jnp.sum(assign_three, axis=1)
    partial_value, masses = (
        lax.psum_scatter(partial_value, "narrow", scatter_dimension=0, tiled=True),
        lax.psum_scatter(masses, "narrow", scatter_dimension=0, tiled=True),
    )
    sums_three, weight_three = lax.psum((partial_value, masses), "wide")
    centre_three = sums_three / jnp.maximum(weight_three, 1.0)[:, None]
    assign_four = jnp.where(
        parents_three[None, :] == jnp.arange(L4, dtype=jnp.int32)[:, None],
        weight_three[None, :],
        0.0,
    )
    sums_four = jnp.dot(
        assign_four,
        centre_three,
        precision=lax.Precision.HIGHEST,
        preferred_element_type=jnp.float32,
    )
    mass_four = jnp.sum(assign_four, axis=1)
    sums_four, mass_four = lax.psum((sums_four, mass_four), "narrow")
    centre_four = sums_four / jnp.maximum(mass_four, 1.0)[:, None]
    return (centre_two, centre_three, centre_four)


def solution(mesh):
    in_specs = (
        P(("wide", "narrow"), None),
        P(("wide", "narrow")),
        P(("wide", "narrow"), None),
        P(("wide", "narrow"), None),
        P(("wide", "narrow"), None),
        P(("wide", "narrow"), None),
        P(("wide", "narrow")),
        P("narrow"),
    )
    out_specs = (P(("wide", "narrow"), None), P("narrow", None), P())
    return jax.shard_map(
        per_device, mesh=mesh, in_specs=in_specs, out_specs=out_specs, check_vma=False
    )
```

```python
import jax
import jax.numpy as jnp
from jax import lax
from jax.experimental import pallas as pl
from jax.experimental.pallas import tpu as pltpu
from jax.sharding import PartitionSpec as P

L4 = 256
CAP = 16
NX, NY, NC, NZ = 4, 4, 2, 8
NW = NX * NY * NC
MESH = pl.DeviceIdType.MESH
SEND_BUFFERS = 2

XY_ORDER = [
    (1, 0), (0, 1), (3, 0), (0, 3), (2, 2), (1, 1), (3, 3), (1, 3),
    (3, 1), (2, 0), (0, 2), (2, 1), (1, 2), (2, 3), (3, 2),
]
WIDE_ORDER = [(dx, dy, dc) for dc in range(NC) for dx, dy in XY_ORDER] + [(0, 0, 1)]


def nt_dot(a, b):
    return lax.dot_general(
        a, b, (((1,), (1,)), ((), ())), preferred_element_type=jnp.float32
    )


def iota(shape, axis):
    return lax.broadcasted_iota(jnp.int32, shape, axis)


def centroid_kernel(
    emb, own, slot, cnt, par2, par3, reseed, donor,
    out2, out3, out4,
    sbuf, rbuf, onehot, pos, lab_send, lab_recv, lab_t, ring_f, ring_b, w_send, w_recv,
    info_z, info_w, tab, req, red_z, red_w, totals, picked,
    part, core_send, core_recv, ring3, ring_d, rows_d, send_d, recv_d, final_d,
    recv_xy, recv_three, three, recv_four, recv_out, acc_four,
    s_sem, r_sem, f_send, f_recv, b_send, b_recv, once, core_s, core_r, s3_sem, r3_sem,
    sd_sem, rd_sem,
):
    rows, width = emb.shape
    half = width // 2
    clusters = out2.shape[0]
    per_z = out3.shape[0]
    mine = per_z // NC
    w = lax.axis_index("wide")
    z = lax.axis_index("narrow")
    x, y, c = w // 8, (w // 2) % 4, w % 2

    def wide_index(d):
        return ((x + d[0]) % NX) * 8 + ((y + d[1]) % NY) * 2 + (c + d[2]) % NC

    def wide_peer(d):
        return (wide_index(d), z)

    def offset(k):
        return k // 8, (k // 2) % 4, k % 2

    def source_of(k):
        dx, dy, dc = offset(k)
        return wide_index((NX - dx, NY - dy, dc))

    def z_peer(k):
        return (w, (z + k) % NZ)

    barrier = pltpu.get_barrier_semaphore()
    for d in WIDE_ORDER:
        pl.semaphore_signal(barrier, inc=1, device_id=wide_peer(d), device_id_type=MESH)
    for k in range(1, NZ):
        pl.semaphore_signal(barrier, inc=1, device_id=z_peer(k), device_id_type=MESH)

    def spread(src, dst, sems, device):
        return pltpu.make_async_remote_copy(
            src_ref=src, dst_ref=dst, send_sem=sems.at[0], recv_sem=sems.at[1],
            device_id=device, device_id_type=MESH,
        )

    def spread_z(src, dst, sems):
        for k in range(1, NZ):
            spread(src, dst.at[k], sems, z_peer(k)).start()

    def join_z(dst, sems):
        at = pl.ds(1, NZ - 1)
        spread(dst.at[at], dst.at[at], sems, z_peer(1)).wait()

    def spread_wide(src, dst, sems):
        for d in WIDE_ORDER:
            k = d[0] * 8 + d[1] * 2 + d[2]
            spread(src, dst.at[k], sems, wide_peer(d)).start()

    def join_wide(dst, sems):
        at = pl.ds(1, NW - 1)
        spread(dst.at[at], dst.at[at], sems, wide_peer((0, 0, 1))).wait()

    sem_info_z, sem_info_w, sem_lab, sem_w = once.at[0], once.at[1], once.at[2], once.at[3]
    sem_red_z, sem_red_w, sem_xy, sem_d = once.at[4], once.at[5], once.at[6], once.at[7]
    sem_three, sem_four, sem_out = once.at[8], once.at[9], once.at[10]

    slots = iota((1, clusters), 1)
    parent = par2[...].astype(jnp.float32)
    hits = [slots == reseed[0:1, k : k + 1] for k in range(2)]
    grands = [jnp.sum(jnp.where(h, parent, 0.0), axis=1, keepdims=True) for h in hits]
    table = parent + jnp.where(hits[0] | hits[1], 1024.0, 0.0)
    lane = iota((1, 128), 1)
    extra = jnp.zeros((1, 128), jnp.float32)
    for i, v in enumerate(
        [donor[0:1, 0:1], donor[0:1, 1:2], grands[0], grands[1], reseed[0:1, 0:1], reseed[0:1, 1:2]]
    ):
        extra = jnp.where(lane == i, v.astype(jnp.float32), extra)
    info_z[0, :, 0:clusters] = jnp.where(iota((NZ, clusters), 0) == z, table, 0.0)
    info_z[0, :, clusters : clusters + 128] = jnp.where(iota((NZ, 128), 0) == z, extra, 0.0)

    owner = own[...]
    target = owner // NZ
    rel = (
        ((target // 8 - x) & 3) * 8 + (((target // 2) - y) & 3) * 2 + ((target - c) & 1)
    )
    step = 256
    upper = (iota((step, step), 0) < iota((step, step), 1)).astype(jnp.bfloat16)
    carry = jnp.zeros((step, 1), jnp.float32)
    for b in range(rows // step):
        cols = slice(b * step, (b + 1) * step)
        hit = iota((step, step), 0) == owner[:, cols]
        mark = hit.astype(jnp.bfloat16)
        earlier = jnp.dot(mark, upper, preferred_element_type=jnp.float32) + carry
        mark32 = hit.astype(jnp.float32)
        rank = jnp.sum(earlier * mark32, axis=0, keepdims=True)
        carry = carry + jnp.sum(mark32, axis=1, keepdims=True)
        pos[0:1, cols] = rel[:, cols] * CAP + rank.astype(jnp.int32)
    pos[1:2, :] = owner % NZ

    pl.semaphore_wait(barrier, NW - 1 + NZ - 1)
    spread_z(info_z.at[0], info_z, sem_info_z)

    places = NW * CAP
    tile = 256

    def fill_onehot(where_row):
        for i in range(places // tile):
            ids = iota((tile, rows), 0) + i * tile
            onehot[i * tile : (i + 1) * tile, :] = (ids == where_row).astype(jnp.bfloat16)

    fill_onehot(pos[0:1, :])
    deep = iota((128, rows), 0)
    z_of = pos[1:2, :]
    labels = jnp.where(
        deep == 2 * z_of, slot[...], jnp.where(deep == 2 * z_of + 1, cnt[...], 0)
    ).astype(jnp.float32).astype(jnp.bfloat16)
    lab_send[...] = nt_dot(onehot[...], labels).astype(jnp.bfloat16)
    lab_recv[0:CAP, :] = lab_send[0:CAP, :]

    def send_wide(src, dst, sem_s, sem_r):
        for d in WIDE_ORDER:
            k = d[0] * 8 + d[1] * 2 + d[2]
            at = pl.ds(k * CAP, CAP)
            pltpu.make_async_remote_copy(
                src_ref=src.at[at], dst_ref=dst.at[at], send_sem=sem_s, recv_sem=sem_r,
                device_id=wide_peer(d), device_id_type=MESH,
            ).start()

    def all_wide(src, dst, sem_s, sem_r):
        at = pl.ds(CAP, places - CAP)
        return pltpu.make_async_remote_copy(
            src_ref=src.at[at], dst_ref=dst.at[at], send_sem=sem_s, recv_sem=sem_r,
            device_id=wide_peer((0, 0, 1)), device_id_type=MESH,
        )

    send_wide(lab_send, lab_recv, sem_lab.at[0], sem_lab.at[1])

    def block_f(t):
        return (z + 2 * NZ - 1 - t) % NZ

    def block_b(t):
        return (z + 1 + t) % NZ

    def pack(t):
        b = lax.rem(t, SEND_BUFFERS)

        @pl.when(t >= SEND_BUFFERS)
        def _():
            all_wide(sbuf.at[b], rbuf.at[t], s_sem.at[b], r_sem.at[t]).wait_send()

        for h, blk in enumerate((block_f(t), block_b(t))):
            fill_onehot(jnp.where(pos[1:2, :] == blk, pos[0:1, :], -1))

            def column(n, _, h=h):
                at = pl.ds(pl.multiple_of(h * half + n * tile, tile), tile)
                sbuf[b, :, at] = jnp.dot(
                    onehot[...], emb[:, at], preferred_element_type=jnp.float32
                ).astype(jnp.bfloat16)
                return 0

            lax.fori_loop(0, half // tile, column, 0)
        rbuf[t, 0:CAP, :] = sbuf[b, 0:CAP, :]

    def send(t):
        b = lax.rem(t, SEND_BUFFERS)
        send_wide(sbuf.at[b], rbuf.at[t], s_sem.at[b], r_sem.at[t])

    join_z(info_z, sem_info_z)
    whole = info_z[0]
    for k in range(1, NZ):
        whole = whole + info_z[k]
    info_w[0] = whole
    spread_wide(info_w.at[0], info_w, sem_info_w)
    pack(0)
    send(0)

    all_wide(lab_send, lab_recv, sem_lab.at[0], sem_lab.at[1]).wait()
    eye = (iota((16, 128), 0) == iota((16, 128), 1)).astype(jnp.bfloat16)
    lab_t[...] = nt_dot(eye, lab_recv[...])

    def matched(blk):
        ids = iota((clusters, places), 0).astype(jnp.float32)
        return ids == lab_t[pl.ds(2 * blk, 1), :], lab_t[pl.ds(2 * blk + 1, 1), :]

    def weigh(k, _):
        hit, counts = matched((z + k) % NZ)
        counts = jnp.broadcast_to(counts, (8, places)).astype(jnp.bfloat16)
        w_send[k] = nt_dot(counts, hit.astype(jnp.float32).astype(jnp.bfloat16))
        return 0

    lax.fori_loop(0, NZ, weigh, 0)
    for k in range(1, NZ):
        spread(w_send.at[k], w_recv.at[k], sem_w, z_peer(k)).start()

    join_wide(info_w, sem_info_w)

    def arrange(k, _):
        src = source_of(k)
        tab[pl.ds(pl.multiple_of(src * NZ, NZ), NZ), :] = info_w[k, :, 0:clusters]
        for zz in range(NZ):
            req[pl.ds(zz * NW + src, 1), :] = info_w[k, zz : zz + 1, clusters : clusters + 128]
        return 0

    lax.fori_loop(0, NW, arrange, 0)
    across = jnp.transpose(tab[...])
    high = jnp.floor(across * (1.0 / 64.0))
    low = (across - 64.0 * high).astype(jnp.bfloat16)
    high = high.astype(jnp.bfloat16)
    for b in range(rows // step):
        cols = slice(b * step, (b + 1) * step)
        mark = (iota((step, step), 0) == own[:, cols]).astype(jnp.bfloat16)
        values = 64.0 * jnp.dot(high, mark, preferred_element_type=jnp.float32) + jnp.dot(
            low, mark, preferred_element_type=jnp.float32
        )
        found = jnp.sum(
            jnp.where(iota((clusters, step), 0) == slot[:, cols], values, 0.0),
            axis=0, keepdims=True,
        ).astype(jnp.int32)
        gone = found >= 1024
        true_parent = jnp.where(gone, found - 1024, found)
        pos[2:3, cols] = jnp.where(gone, -1, true_parent)
        pos[3:4, cols] = true_parent

    devices = NW * NZ
    place = iota((devices, 1), 0)
    owner_of = (place % NW) * NZ + place // NW
    ident = own[...] * clusters + slot[...]
    for k in range(2):
        asked = owner_of * clusters + req[:, 4 + k : 5 + k].astype(jnp.int32)
        onehot[k * devices : (k + 1) * devices, :] = (asked == ident).astype(jnp.bfloat16)
    counts32 = cnt[...].astype(jnp.float32)
    counts8 = jnp.broadcast_to(counts32, (8, rows)).astype(jnp.bfloat16)
    true_parent = pos[3:4, :]
    by_z = jnp.where(iota((8, rows), 0) == true_parent // per_z, counts32, 0.0).astype(jnp.bfloat16)
    inside = (iota((per_z, rows), 0) == true_parent % per_z).astype(jnp.bfloat16)
    red_z[0, :, 0 : 2 * devices] = nt_dot(counts8, onehot[...])
    red_z[0, :, 2 * devices : 2 * devices + per_z] = nt_dot(by_z, inside)
    spread_z(red_z.at[0], red_z, sem_red_z)

    def reduce_weights_z():
        join_z(red_z, sem_red_z)
        total = red_z[0]
        for k in range(1, NZ):
            total = total + red_z[k]
        red_w[0] = total
        spread_wide(red_w.at[0], red_w, sem_red_w)

    def reduce_weights_wide():
        join_wide(red_w, sem_red_w)
        total = red_w[0].astype(jnp.int32)
        for k in range(1, NW):
            total = total + red_w[k].astype(jnp.int32)
        totals[...] = total.astype(jnp.float32)

    def pick_donors():
        first = (w * NZ + z) * rows
        for k in range(2):
            local = req[:, k : k + 1].astype(jnp.int32) - first
            onehot[k * devices : (k + 1) * devices, :] = (
                iota((devices, rows), 1) == local
            ).astype(jnp.bfloat16)

        def column(n, _):
            at = pl.ds(pl.multiple_of(n * tile, tile), tile)
            picked[:, at] = jnp.dot(
                onehot[...], emb[:, at], preferred_element_type=jnp.float32
            ).astype(jnp.bfloat16)
            return 0

        lax.fori_loop(0, width // tile, column, 0)

    def core_copy(s):
        b = lax.rem(s, 2)
        return pltpu.make_async_remote_copy(
            src_ref=core_send.at[b], dst_ref=core_recv.at[s],
            send_sem=core_s.at[b], recv_sem=core_r.at[s],
            device_id=wide_peer((0, 0, 1)), device_id_type=MESH,
        )

    def three_terms(value):
        first = value.astype(jnp.bfloat16)
        rest = value - first.astype(jnp.float32)
        second = rest.astype(jnp.bfloat16)
        return first, second, (rest - second.astype(jnp.float32)).astype(jnp.bfloat16)

    def local_three(s):
        b = lax.rem(s, 2)

        @pl.when(s >= 2)
        def _():
            core_copy(s - 2).wait_send()

        grand_rows = jnp.transpose(req[...])
        for h, blk in enumerate((block_f(s), block_b(s))):
            base = jnp.where(
                iota((per_z, rows), 0) + per_z * blk == pos[2:3, :], cnt[...], 0
            ).astype(jnp.float32).astype(jnp.bfloat16)
            ids = (iota((per_z, devices), 0) + per_z * blk).astype(jnp.float32)
            heavy = [
                three_terms(
                    jnp.where(
                        ids == grand_rows[2 + k : 3 + k, :],
                        totals[0:1, k * devices : (k + 1) * devices],
                        0.0,
                    )
                )
                for k in range(2)
            ]
            for n in range(half // tile):
                at = slice(h * half + n * tile, h * half + (n + 1) * tile)
                value = jnp.dot(base, emb[:, at], preferred_element_type=jnp.float32)
                for k in range(2):
                    for term in heavy[k]:
                        value = value + jnp.dot(
                            term,
                            picked[k * devices : (k + 1) * devices, at],
                            preferred_element_type=jnp.float32,
                        )
                part[b, h, :, n * tile : (n + 1) * tile] = value
            core_send[b, h] = part[b, h, pl.ds(pl.multiple_of((1 - c) * mine, mine), mine), :]
        core_copy(s).start()

    def ring3_copy(h, s):
        return pltpu.make_async_remote_copy(
            src_ref=ring3.at[h, s], dst_ref=ring3.at[h, s + 1],
            send_sem=s3_sem.at[h, s], recv_sem=r3_sem.at[h, s + 1],
            device_id=z_peer((1, NZ - 1)[h]), device_id_type=MESH,
        )

    def ring_d_copy(h, s):
        return pltpu.make_async_remote_copy(
            src_ref=ring_d.at[h, s], dst_ref=ring_d.at[h, s + 1],
            send_sem=sd_sem.at[h, s], recv_sem=rd_sem.at[h, s + 1],
            device_id=z_peer((1, NZ - 1)[h]), device_id_type=MESH,
        )

    def step_three(s):
        @pl.when(s < NZ - 1)
        def _():
            local_three(s + 1)

        b = lax.rem(s, 2)
        core_copy(s).wait_recv()
        for h, blk in enumerate((block_f(s), block_b(s))):
            at = pl.ds(pl.multiple_of(c * mine, mine), mine)
            value = part[b, h, at, :] + core_recv[s, h]
            chosen = picked[pl.ds(pl.multiple_of(h * devices + blk * NW, NW), NW), :]

            @pl.when(s == 0)
            def _(h=h, value=value, chosen=chosen):
                ring3[h, s] = value
                ring_d[h, s] = chosen

            @pl.when(s > 0)
            def _(h=h, value=value, chosen=chosen):
                ring3_copy(h, s - 1).wait_recv()
                ring3[h, s] += value
                ring_d_copy(h, s - 1).wait_recv()
                ring_d[h, s] = (
                    ring_d[h, s].astype(jnp.float32) + chosen.astype(jnp.float32)
                ).astype(jnp.bfloat16)

            @pl.when(s < NZ - 1)
            def _(h=h):
                ring3_copy(h, s).start()
                ring_d_copy(h, s).start()

    quarter = width // 4

    def piece(xx, yy):
        i = xx * NY + yy
        return ring3.at[i // 8, NZ - 1, pl.ds(pl.multiple_of((i % 8) * 8, 8), 8)]

    def send_three_and_donors():
        recv_xy[0] = piece(x, y)[...]
        for dx, dy in XY_ORDER:
            spread(
                piece((x + dx) % NX, (y + dy) % NY), recv_xy.at[dx * NY + dy], sem_xy,
                wide_peer((dx, dy, 0)),
            ).start()
        for h in range(2):
            rows_d[h] = ring_d[h, NZ - 1].astype(jnp.float32)

        def lay(k, _):
            to = wide_index(offset(k))
            for h in range(2):
                for j in range(4):
                    send_d[k, 4 * h + j : 4 * h + j + 1, :] = rows_d[
                        h, pl.ds(to, 1), j * quarter : (j + 1) * quarter
                    ]
            return 0

        lax.fori_loop(0, NW, lay, 0)
        recv_d[0] = send_d[0]
        for d in WIDE_ORDER:
            k = d[0] * 8 + d[1] * 2 + d[2]
            spread(send_d.at[k], recv_d.at[k], sem_d, wide_peer(d)).start()

    def join_three_and_donors():
        at = pl.ds(1, NX * NY - 1)
        spread(recv_xy.at[at], recv_xy.at[at], sem_xy, wide_peer((0, 1, 0))).wait()
        total = recv_xy[0]
        for k in range(1, NX * NY):
            total = total + recv_xy[k]
        recv_three[0] = total
        join_wide(recv_d, sem_d)
        total = recv_d[0]
        for k in range(1, NW):
            total = total + recv_d[k]
        final_d[...] = total

    def finish_three():
        join_wide(recv_three, sem_three)

        def lay(k, _):
            src = source_of(k)
            i = src // 2
            row = (src % 2) * mine + (i % 8) * 8
            three[i // 8, pl.ds(pl.multiple_of(row, 8), 8), :] = recv_three[k]
            return 0

        lax.fori_loop(0, NW, lay, 0)
        masses = totals[:, 2 * devices : 2 * devices + per_z]
        mass_row = jnp.sum(
            jnp.where(iota((8, per_z), 0) == z, masses, 0.0), axis=0, keepdims=True
        )
        diagonal = iota((per_z, per_z), 0) == iota((per_z, per_z), 1)
        mass = jnp.sum(jnp.where(diagonal, mass_row, 0.0), axis=1, keepdims=True)
        mass = jnp.maximum(mass, 1.0)
        chosen = par3[...] == iota((8, per_z), 0) + 8 * w
        pick = chosen.astype(jnp.float32).astype(jnp.bfloat16)
        for h in range(2):
            out3[:, h * half : (h + 1) * half] = three[h] / mass
            total = jnp.zeros((8, half), jnp.float32)
            for term in three_terms(three[h]):
                total = total + jnp.dot(pick, term, preferred_element_type=jnp.float32)
            recv_four[0, :, h * half : (h + 1) * half] = total
        mass_four = jnp.sum(jnp.where(chosen, mass_row, 0.0), axis=1, keepdims=True)
        recv_four[0, :, width : width + 128] = jnp.broadcast_to(mass_four, (8, 128))
        spread_z(recv_four.at[0], recv_four, sem_four)

    def send_four():
        join_z(recv_four, sem_four)
        acc_four[...] = recv_four[z]
        for zz in range(1, NZ):
            acc_four[...] += recv_four[(z + NZ - zz) % NZ]
        mass = jnp.maximum(acc_four[:, width : width + 1], 1.0)
        recv_out[0] = acc_four[:, 0:width] / mass
        spread_wide(recv_out.at[0], recv_out, sem_out)

    def finish_four():
        join_wide(recv_out, sem_out)

        def lay(k, _):
            out4[pl.ds(pl.multiple_of(source_of(k) * 8, 8), 8), :] = recv_out[k]
            return 0

        lax.fori_loop(0, NW, lay, 0)

    def ring_copy(ring, t, sems, k):
        return pltpu.make_async_remote_copy(
            src_ref=ring.at[t], dst_ref=ring.at[t + 1],
            send_sem=sems[0].at[t], recv_sem=sems[1].at[t + 1],
            device_id=z_peer(k), device_id_type=MESH,
        )

    rings = (
        (ring_f, (f_send, f_recv), 1, block_f),
        (ring_b, (b_send, b_recv), NZ - 1, block_b),
    )

    def reduce_stage(t):
        all_wide(sbuf.at[0], rbuf.at[t], s_sem.at[0], r_sem.at[t]).wait_recv()
        for h, (ring, sems, k, block) in enumerate(rings):
            hit, counts = matched(block(t))
            assign = jnp.where(hit, counts, 0.0).astype(jnp.bfloat16)

            @pl.when(t > 0)
            def _(ring=ring, sems=sems, k=k):
                ring_copy(ring, t - 1, sems, k).wait_recv()

            for n in range(half // tile):
                at = slice(n * tile, (n + 1) * tile)
                value = jnp.dot(
                    assign,
                    rbuf[t, :, h * half + n * tile : h * half + (n + 1) * tile],
                    preferred_element_type=jnp.float32,
                )

                @pl.when(t == 0)
                def _(ring=ring, at=at, value=value):
                    ring[t, :, at] = value

                @pl.when(t > 0)
                def _(ring=ring, at=at, value=value):
                    ring[t, :, at] += value

            @pl.when(t < NZ - 1)
            def _(ring=ring, sems=sems, k=k):
                ring_copy(ring, t, sems, k).start()

    def at_stage(t, which, work):
        pl.when(t == which)(work)

    def stage(t, _):
        @pl.when(t < NZ - 1)
        def _():
            pack(t + 1)

        at_stage(t, 0, reduce_weights_z)

        @pl.when((t >= 1) & (t <= 4))
        def _():
            step_three(2 * t - 2)

        at_stage(t, 5, send_three_and_donors)
        at_stage(t, 6, lambda: spread_wide(recv_three.at[0], recv_three, sem_three))
        at_stage(t, 7, send_four)

        @pl.when(t < NZ - 1)
        def _():
            send(t + 1)

        reduce_stage(t)

        @pl.when(t == 0)
        def _():
            reduce_weights_wide()
            pick_donors()
            local_three(0)

        @pl.when((t >= 1) & (t <= 4))
        def _():
            step_three(2 * t - 1)

        at_stage(t, 5, join_three_and_donors)
        at_stage(t, 6, finish_three)
        return 0

    lax.fori_loop(0, NZ, stage, 0)

    others = pl.ds(1, NZ - 1)
    spread(w_send.at[others], w_recv.at[others], sem_w, z_peer(1)).wait()
    total = w_send[0]
    for k in range(1, NZ):
        total = total + w_recv[k]
    diagonal = iota((clusters, clusters), 0) == iota((clusters, clusters), 1)
    mass = jnp.sum(jnp.where(diagonal, total[0:1, :], 0.0), axis=1, keepdims=True)
    mass = jnp.maximum(mass, 1.0)
    seeded = [iota((clusters, 1), 0) == reseed[0:1, k : k + 1] for k in range(2)]
    for j in range(4):
        ring = rings[j // 2][0]
        at = (j % 2) * quarter
        value = ring[NZ - 1, :, at : at + quarter] / mass
        for k in range(2):
            value = jnp.where(seeded[k], final_d[4 * k + j : 4 * k + j + 1, :], value)
        out2[:, j * quarter : (j + 1) * quarter] = value

    finish_four()
    for b in range(SEND_BUFFERS):
        all_wide(sbuf.at[b], rbuf.at[0], s_sem.at[b], r_sem.at[0]).wait_send()
    for b in range(2):
        core_copy(b).wait_send()

    def drain(t, _):
        for h, (ring, sems, k, block) in enumerate(rings):
            ring_copy(ring, t, sems, k).wait_send()
            ring3_copy(h, t).wait_send()
            ring_d_copy(h, t).wait_send()
        return 0

    lax.fori_loop(0, NZ - 1, drain, 0)


def per_device(
    embeddings,
    point_counts,
    owner_ids,
    owner_slots,
    reseed_slots,
    donor_ids,
    parents_two,
    parents_three,
):
    rows, width = embeddings.shape
    clusters = parents_two.shape[0]
    per_z = parents_three.shape[0]
    half = width // 2
    places = NW * CAP
    devices = NW * NZ
    f32, bf16 = jnp.float32, jnp.bfloat16
    vmem = pl.BlockSpec(memory_space=pltpu.VMEM)
    dma = pltpu.SemaphoreType.DMA
    return pl.pallas_call(
        centroid_kernel,
        out_shape=(
            jax.ShapeDtypeStruct((clusters, width), f32),
            jax.ShapeDtypeStruct((per_z, width), f32),
            jax.ShapeDtypeStruct((L4, width), f32),
        ),
        in_specs=[vmem] * 8,
        out_specs=(vmem,) * 3,
        scratch_shapes=[
            pltpu.VMEM((SEND_BUFFERS, places, width), bf16),
            pltpu.VMEM((NZ, places, width), bf16),
            pltpu.VMEM((places, rows), bf16),
            pltpu.VMEM((8, rows), jnp.int32),
            pltpu.VMEM((places, 128), bf16),
            pltpu.VMEM((places, 128), bf16),
            pltpu.VMEM((16, places), f32),
            pltpu.VMEM((NZ, clusters, half), f32),
            pltpu.VMEM((NZ, clusters, half), f32),
            pltpu.VMEM((NZ, 8, clusters), f32),
            pltpu.VMEM((NZ, 8, clusters), f32),
            pltpu.VMEM((NZ, NZ, clusters + 128), f32),
            pltpu.VMEM((NW, NZ, clusters + 128), f32),
            pltpu.VMEM((devices, clusters), f32),
            pltpu.VMEM((devices, 128), f32),
            pltpu.VMEM((NZ, 8, 2 * devices + per_z), f32),
            pltpu.VMEM((NW, 8, 2 * devices + per_z), f32),
            pltpu.VMEM((8, 2 * devices + per_z), f32),
            pltpu.VMEM((2 * devices, width), bf16),
            pltpu.VMEM((2, 2, per_z, half), f32),
            pltpu.VMEM((2, 2, per_z // NC, half), f32),
            pltpu.VMEM((NZ, 2, per_z // NC, half), f32),
            pltpu.VMEM((2, NZ, per_z // NC, half), f32),
            pltpu.VMEM((2, NZ, NW, width), bf16),
            pltpu.VMEM((2, NW, width), f32),
            pltpu.VMEM((NW, 8, width // 4), f32),
            pltpu.VMEM((NW, 8, width // 4), f32),
            pltpu.VMEM((8, width // 4), f32),
            pltpu.VMEM((NX * NY, 8, half), f32),
            pltpu.VMEM((NW, 8, half), f32),
            pltpu.VMEM((2, per_z, half), f32),
            pltpu.VMEM((NZ, 8, width + 128), f32),
            pltpu.VMEM((NW, 8, width), f32),
            pltpu.VMEM((8, width + 128), f32),
            dma((SEND_BUFFERS,)),
            dma((NZ,)),
            dma((NZ,)),
            dma((NZ,)),
            dma((NZ,)),
            dma((NZ,)),
            dma((11, 2)),
            dma((2,)),
            dma((NZ,)),
            dma((2, NZ)),
            dma((2, NZ)),
            dma((2, NZ)),
            dma((2, NZ)),
        ],
        compiler_params=pltpu.CompilerParams(
            collective_id=0, has_side_effects=True, vmem_limit_bytes=63 * 2**20
        ),
    )(
        embeddings,
        owner_ids.reshape(1, rows),
        owner_slots.reshape(1, rows),
        point_counts.reshape(1, rows),
        parents_two.reshape(1, clusters),
        parents_three.reshape(1, per_z),
        reseed_slots,
        donor_ids,
    )


def solution(mesh):
    in_specs = (
        P(("wide", "narrow"), None),
        P(("wide", "narrow")),
        P(("wide", "narrow"), None),
        P(("wide", "narrow"), None),
        P(("wide", "narrow"), None),
        P(("wide", "narrow"), None),
        P(("wide", "narrow")),
        P("narrow"),
    )
    out_specs = (P(("wide", "narrow"), None), P("narrow", None), P())
    return jax.shard_map(
        per_device, mesh=mesh, in_specs=in_specs, out_specs=out_specs, check_vma=False
    )
```

```python
import jax
import jax.numpy as jnp
from jax import lax
from jax.experimental import pallas as pl
from jax.experimental.pallas import tpu as pltpu
from jax.sharding import PartitionSpec as P

L4 = 256
CAP = 16
NX, NY, NC, NZ = 4, 4, 2, 8
NW = NX * NY * NC
MESH = pl.DeviceIdType.MESH
TOP = 32767.0
SEND_BUFFERS = 3

XY_ORDER = [
    (1, 0), (0, 1), (3, 0), (0, 3), (2, 2), (1, 1), (3, 3), (1, 3),
    (3, 1), (2, 0), (0, 2), (2, 1), (1, 2), (2, 3), (3, 2),
]
WIDE_ORDER = [(dx, dy, dc) for dc in range(NC) for dx, dy in XY_ORDER] + [(0, 0, 1)]


def rel_of(d):
    return (d[2] * NX + d[0]) * NY + d[1]


def nt_dot(a, b):
    return lax.dot_general(
        a, b, (((1,), (1,)), ((), ())), preferred_element_type=jnp.float32
    )


def iota(shape, axis):
    return lax.broadcasted_iota(jnp.int32, shape, axis)


def centroid_kernel(
    emb_hbm, own, slot, cnt, par2, par3, reseed, donor,
    out2, out3, out4,
    emb, sbuf, rbuf, onehot, pos, lab_send, lab_recv, lab_t, ring_q, ring_s, acc, turn, w_send, w_recv,
    info_z, info_w, tab, req, red_z, red_w, red_c, totals, picked, donors_c,
    part, core_send, core_recv, ring3, ring_d, rows_d, send_d, recv_d, final_d,
    recv_xy, recv_three, three, recv_four, recv_out, acc_four,
    load_sem, s_sem, r_sem, q_send, q_recv, sc_send, sc_recv, once, core_s, core_r, s3_sem, r3_sem,
    sd_sem, rd_sem,
):
    load = pltpu.make_async_copy(emb_hbm, emb, load_sem.at[0])
    load.start()
    rows, width = emb.shape
    half = width // 2
    clusters = out2.shape[0]
    per_z = out3.shape[0]
    mine = per_z // NC
    w = lax.axis_index("wide")
    z = lax.axis_index("narrow")
    x, y, c = w // 8, (w // 2) % 4, w % 2

    def wide_index(d):
        return ((x + d[0]) % NX) * 8 + ((y + d[1]) % NY) * 2 + (c + d[2]) % NC

    def wide_peer(d):
        return (wide_index(d), z)

    def offset(k):
        return (k // NY) % NX, k % NY, k // (NX * NY)

    def source_of(k):
        dx, dy, dc = offset(k)
        return wide_index((NX - dx, NY - dy, dc))

    def z_peer(k):
        return (w, (z + k) % NZ)

    barrier = pltpu.get_barrier_semaphore()
    for d in WIDE_ORDER:
        pl.semaphore_signal(barrier, inc=1, device_id=wide_peer(d), device_id_type=MESH)
    for k in range(1, NZ):
        pl.semaphore_signal(barrier, inc=1, device_id=z_peer(k), device_id_type=MESH)

    def spread(src, dst, sems, device):
        return pltpu.make_async_remote_copy(
            src_ref=src, dst_ref=dst, send_sem=sems.at[0], recv_sem=sems.at[1],
            device_id=device, device_id_type=MESH,
        )

    def spread_z(src, dst, sems):
        for k in range(1, NZ):
            spread(src, dst.at[k], sems, z_peer(k)).start()

    def join_z(dst, sems):
        at = pl.ds(1, NZ - 1)
        spread(dst.at[at], dst.at[at], sems, z_peer(1)).wait()

    def spread_xy(src, dst, sems):
        for dx, dy in XY_ORDER:
            spread(src, dst.at[dx * NY + dy], sems, wide_peer((dx, dy, 0))).start()

    def join_xy(dst, sems):
        at = pl.ds(1, NX * NY - 1)
        spread(dst.at[at], dst.at[at], sems, wide_peer((0, 1, 0))).wait()

    def to_core(dst, sems):
        here, there = pl.ds(0, NX * NY), pl.ds(NX * NY, NX * NY)
        return spread(dst.at[here], dst.at[there], sems, wide_peer((0, 0, 1)))

    sem_info_z, sem_info_w, sem_lab, sem_w = once.at[0], once.at[1], once.at[2], once.at[3]
    sem_red_z, sem_red_w, sem_xy, sem_d = once.at[4], once.at[5], once.at[6], once.at[7]
    sem_three, sem_four, sem_out = once.at[8], once.at[9], once.at[10]
    sem_info_c, sem_red_c, sem_three_c = once.at[11], once.at[12], once.at[13]
    sem_out_c, sem_donors_c = once.at[14], once.at[15]

    slots = iota((1, clusters), 1)
    parent = par2[...].astype(jnp.float32)
    hits = [slots == reseed[0:1, k : k + 1] for k in range(2)]
    grands = [jnp.sum(jnp.where(h, parent, 0.0), axis=1, keepdims=True) for h in hits]
    table = parent + jnp.where(hits[0] | hits[1], 1024.0, 0.0)
    lane = iota((1, 128), 1)
    extra = jnp.zeros((1, 128), jnp.float32)
    for i, v in enumerate(
        [donor[0:1, 0:1], donor[0:1, 1:2], grands[0], grands[1], reseed[0:1, 0:1], reseed[0:1, 1:2]]
    ):
        extra = jnp.where(lane == i, v.astype(jnp.float32), extra)
    info_z[0, :, 0:clusters] = jnp.where(iota((NZ, clusters), 0) == z, table, 0.0)
    info_z[0, :, clusters : clusters + 128] = jnp.where(iota((NZ, 128), 0) == z, extra, 0.0)

    owner = own[...]
    target = owner // NZ
    rel = (
        ((target - c) & 1) * 16 + ((target // 8 - x) & 3) * 4 + (((target // 2) - y) & 3)
    )
    step = 256
    upper = (iota((step, step), 0) < iota((step, step), 1)).astype(jnp.bfloat16)
    carry = jnp.zeros((step, 1), jnp.float32)
    for b in range(rows // step):
        cols = slice(b * step, (b + 1) * step)
        hit = iota((step, step), 0) == owner[:, cols]
        mark = hit.astype(jnp.bfloat16)
        earlier = jnp.dot(mark, upper, preferred_element_type=jnp.float32) + carry
        mark32 = hit.astype(jnp.float32)
        rank = jnp.sum(earlier * mark32, axis=0, keepdims=True)
        carry = carry + jnp.sum(mark32, axis=1, keepdims=True)
        pos[0:1, cols] = rel[:, cols] * CAP + rank.astype(jnp.int32)
    pos[1:2, :] = owner % NZ

    pl.semaphore_wait(barrier, NW - 1 + NZ - 1)
    spread_z(info_z.at[0], info_z, sem_info_z)

    places = NW * CAP
    tile = 256

    def fill_onehot(where_row):
        for i in range(places // tile):
            ids = iota((tile, rows), 0) + i * tile
            onehot[i * tile : (i + 1) * tile, :] = (ids == where_row).astype(jnp.bfloat16)

    fill_onehot(pos[0:1, :])
    deep = iota((128, rows), 0)
    z_of = pos[1:2, :]
    labels = jnp.where(
        deep == 2 * z_of, slot[...], jnp.where(deep == 2 * z_of + 1, cnt[...], 0)
    ).astype(jnp.float32).astype(jnp.bfloat16)
    lab_send[...] = nt_dot(onehot[...], labels).astype(jnp.bfloat16)
    lab_recv[0:CAP, :] = lab_send[0:CAP, :]

    def send_wide(src, dst, sem_s, sem_r):
        for d in WIDE_ORDER:
            at = pl.ds(rel_of(d) * CAP, CAP)
            pltpu.make_async_remote_copy(
                src_ref=src.at[at], dst_ref=dst.at[at], send_sem=sem_s, recv_sem=sem_r,
                device_id=wide_peer(d), device_id_type=MESH,
            ).start()

    def all_wide(src, dst, sem_s, sem_r):
        at = pl.ds(CAP, places - CAP)
        return pltpu.make_async_remote_copy(
            src_ref=src.at[at], dst_ref=dst.at[at], send_sem=sem_s, recv_sem=sem_r,
            device_id=wide_peer((0, 0, 1)), device_id_type=MESH,
        )

    send_wide(lab_send, lab_recv, sem_lab.at[0], sem_lab.at[1])

    def block_f(t):
        return (z + 2 * NZ - 1 - t) % NZ

    def block_b(t):
        return (z + 1 + t) % NZ

    def pack(t):
        b = lax.rem(t, SEND_BUFFERS)

        @pl.when(t >= SEND_BUFFERS)
        def _():
            all_wide(sbuf.at[b], rbuf.at[t], s_sem.at[b], r_sem.at[t]).wait_send()

        for h, blk in enumerate((block_f(t), block_b(t))):
            fill_onehot(jnp.where(pos[1:2, :] == blk, pos[0:1, :], -1))

            def column(n, _, h=h):
                at = pl.ds(pl.multiple_of(h * half + n * tile, tile), tile)
                sbuf[b, :, at] = jnp.dot(
                    onehot[...], emb[:, at], preferred_element_type=jnp.float32
                ).astype(jnp.bfloat16)
                return 0

            lax.fori_loop(0, half // tile, column, 0)
        rbuf[t, 0:CAP, :] = sbuf[b, 0:CAP, :]

    def send(t):
        b = lax.rem(t, SEND_BUFFERS)
        send_wide(sbuf.at[b], rbuf.at[t], s_sem.at[b], r_sem.at[t])

    load.wait()
    pack(0)
    join_z(info_z, sem_info_z)
    whole = info_z[0]
    for k in range(1, NZ):
        whole = whole + info_z[k]
    info_w[0] = whole
    spread_xy(info_w.at[0], info_w, sem_info_w)
    send(0)

    turn[...] = jnp.zeros(turn.shape, jnp.float32)
    join_xy(info_w, sem_info_w)
    to_core(info_w, sem_info_c).start()
    all_wide(lab_send, lab_recv, sem_lab.at[0], sem_lab.at[1]).wait()
    eye = (iota((16, 128), 0) == iota((16, 128), 1)).astype(jnp.bfloat16)
    lab_t[...] = nt_dot(eye, lab_recv[...])

    def matched(blk):
        ids = iota((clusters, places), 0).astype(jnp.float32)
        return ids == lab_t[pl.ds(2 * blk, 1), :], lab_t[pl.ds(2 * blk + 1, 1), :]

    def weigh(k, _):
        hit, counts = matched((z + k) % NZ)
        counts = jnp.broadcast_to(counts, (8, places)).astype(jnp.bfloat16)
        w_send[k] = nt_dot(counts, hit.astype(jnp.float32).astype(jnp.bfloat16))
        return 0

    lax.fori_loop(0, NZ, weigh, 0)
    for k in range(1, NZ):
        spread(w_send.at[k], w_recv.at[k], sem_w, z_peer(k)).start()

    to_core(info_w, sem_info_c).wait()

    devices = NW * NZ

    def arrange(k, _):
        src = source_of(k)
        tab[pl.ds(pl.multiple_of(src * NZ, NZ), NZ), :] = info_w[k, :, 0:clusters]
        for zz in range(NZ):
            row = (src % 2) * (devices // NC) + zz * (NX * NY) + src // 2
            req[pl.ds(row, 1), :] = info_w[k, zz : zz + 1, clusters : clusters + 128]
        return 0

    lax.fori_loop(0, NW, arrange, 0)
    across = jnp.transpose(tab[...])
    high = jnp.floor(across * (1.0 / 64.0))
    low = (across - 64.0 * high).astype(jnp.bfloat16)
    high = high.astype(jnp.bfloat16)
    for b in range(rows // step):
        cols = slice(b * step, (b + 1) * step)
        mark = (iota((step, step), 0) == own[:, cols]).astype(jnp.bfloat16)
        values = 64.0 * jnp.dot(high, mark, preferred_element_type=jnp.float32) + jnp.dot(
            low, mark, preferred_element_type=jnp.float32
        )
        found = jnp.sum(
            jnp.where(iota((clusters, step), 0) == slot[:, cols], values, 0.0),
            axis=0, keepdims=True,
        ).astype(jnp.int32)
        gone = found >= 1024
        true_parent = jnp.where(gone, found - 1024, found)
        pos[2:3, cols] = jnp.where(gone, -1, true_parent)
        pos[3:4, cols] = true_parent

    place = iota((devices, 1), 0)
    owner_of = ((place % 16) * NC + place // 128) * NZ + (place // 16) % NZ
    ident = own[...] * clusters + slot[...]
    for k in range(2):
        asked = owner_of * clusters + req[:, 4 + k : 5 + k].astype(jnp.int32)
        onehot[k * devices : (k + 1) * devices, :] = (asked == ident).astype(jnp.bfloat16)
    counts32 = cnt[...].astype(jnp.float32)
    counts8 = jnp.broadcast_to(counts32, (8, rows)).astype(jnp.bfloat16)
    true_parent = pos[3:4, :]
    by_z = jnp.where(iota((8, rows), 0) == true_parent // per_z, counts32, 0.0).astype(jnp.bfloat16)
    inside = (iota((per_z, rows), 0) == true_parent % per_z).astype(jnp.bfloat16)
    asked_weights = nt_dot(counts8, onehot[...])
    folded = jnp.zeros((8, 128), jnp.float32)
    for i in range(2 * devices // 128):
        folded = jnp.where(
            iota((8, 128), 0) == i, asked_weights[:, i * 128 : (i + 1) * 128], folded
        )
    red_z[0, :, 0:128] = folded
    red_z[0, :, 128 : 128 + per_z] = nt_dot(by_z, inside)
    spread_z(red_z.at[0], red_z, sem_red_z)

    def reduce_weights_z():
        join_z(red_z, sem_red_z)
        total = red_z[0]
        for k in range(1, NZ):
            total = total + red_z[k]
        red_w[0] = total
        spread_xy(red_w.at[0], red_w, sem_red_w)

    def reduce_weights_wide():
        join_xy(red_w, sem_red_w)
        total = red_w[0].astype(jnp.int32)
        for k in range(1, NX * NY):
            total = total + red_w[k].astype(jnp.int32)
        red_c[0] = total
        swap = spread(red_c.at[0], red_c.at[1], sem_red_c, wide_peer((0, 0, 1)))
        swap.start()
        swap.wait()
        total = (total + red_c[1]).astype(jnp.float32)
        for i in range(2 * devices // 128):
            totals[0:1, i * 128 : (i + 1) * 128] = total[i : i + 1, 0:128]
        totals[:, 2 * devices : 2 * devices + per_z] = total[:, 128 : 128 + per_z]

    def pick_donors():
        first = (w * NZ + z) * rows
        for k in range(2):
            local = req[:, k : k + 1].astype(jnp.int32) - first
            onehot[k * devices : (k + 1) * devices, :] = (
                iota((devices, rows), 1) == local
            ).astype(jnp.bfloat16)

        def column(n, _):
            at = pl.ds(pl.multiple_of(n * tile, tile), tile)
            picked[:, at] = jnp.dot(
                onehot[...], emb[:, at], preferred_element_type=jnp.float32
            ).astype(jnp.bfloat16)
            return 0

        lax.fori_loop(0, width // tile, column, 0)
        for k in range(2):
            donors_copy(k).start()

    def donors_copy(k):
        at = pl.ds(pl.multiple_of(k * devices + (1 - c) * 128, 128), 128)
        return spread(picked.at[at], donors_c.at[k], sem_donors_c, wide_peer((0, 0, 1)))

    def core_copy(s):
        b = lax.rem(s, 2)
        return pltpu.make_async_remote_copy(
            src_ref=core_send.at[b], dst_ref=core_recv.at[s],
            send_sem=core_s.at[b], recv_sem=core_r.at[s],
            device_id=wide_peer((0, 0, 1)), device_id_type=MESH,
        )

    def three_terms(value):
        first = value.astype(jnp.bfloat16)
        rest = value - first.astype(jnp.float32)
        second = rest.astype(jnp.bfloat16)
        return first, second, (rest - second.astype(jnp.float32)).astype(jnp.bfloat16)

    def local_three(s):
        b = lax.rem(s, 2)

        @pl.when(s >= 2)
        def _():
            core_copy(s - 2).wait_send()

        grand_rows = jnp.transpose(req[...])
        for h, blk in enumerate((block_f(s), block_b(s))):
            base = jnp.where(
                iota((per_z, rows), 0) + per_z * blk == pos[2:3, :], cnt[...], 0
            ).astype(jnp.float32).astype(jnp.bfloat16)
            ids = (iota((per_z, devices), 0) + per_z * blk).astype(jnp.float32)
            heavy = [
                three_terms(
                    jnp.where(
                        ids == grand_rows[2 + k : 3 + k, :],
                        totals[0:1, k * devices : (k + 1) * devices],
                        0.0,
                    )
                )
                for k in range(2)
            ]
            for n in range(half // tile):
                at = slice(h * half + n * tile, h * half + (n + 1) * tile)
                value = jnp.dot(base, emb[:, at], preferred_element_type=jnp.float32)
                for k in range(2):
                    for term in heavy[k]:
                        value = value + jnp.dot(
                            term,
                            picked[k * devices : (k + 1) * devices, at],
                            preferred_element_type=jnp.float32,
                        )
                part[b, h, :, n * tile : (n + 1) * tile] = value
            core_send[b, h] = part[b, h, pl.ds(pl.multiple_of((1 - c) * mine, mine), mine), :]
        core_copy(s).start()

    def ring3_copy(h, s):
        return pltpu.make_async_remote_copy(
            src_ref=ring3.at[h, s], dst_ref=ring3.at[h, s + 1],
            send_sem=s3_sem.at[h, s], recv_sem=r3_sem.at[h, s + 1],
            device_id=z_peer((1, NZ - 1)[h]), device_id_type=MESH,
        )

    def ring_d_copy(h, s):
        return pltpu.make_async_remote_copy(
            src_ref=ring_d.at[h, s], dst_ref=ring_d.at[h, s + 1],
            send_sem=sd_sem.at[h, s], recv_sem=rd_sem.at[h, s + 1],
            device_id=z_peer((1, NZ - 1)[h]), device_id_type=MESH,
        )

    def step_three(s):
        @pl.when(s < NZ - 1)
        def _():
            local_three(s + 1)

        b = lax.rem(s, 2)
        core_copy(s).wait_recv()
        for h, blk in enumerate((block_f(s), block_b(s))):
            at = pl.ds(pl.multiple_of(c * mine, mine), mine)
            value = part[b, h, at, :] + core_recv[s, h]
            at = pl.ds(pl.multiple_of(h * devices + c * 128 + blk * 16, 16), 16)
            chosen = (
                picked[at, :].astype(jnp.float32)
                + donors_c[h, pl.ds(pl.multiple_of(blk * 16, 16), 16), :].astype(jnp.float32)
            ).astype(jnp.bfloat16)

            @pl.when(s == 0)
            def _(h=h, value=value, chosen=chosen):
                ring3[h, s] = value
                ring_d[h, s] = chosen

            @pl.when(s > 0)
            def _(h=h, value=value, chosen=chosen):
                ring3_copy(h, s - 1).wait_recv()
                ring3[h, s] += value
                ring_d_copy(h, s - 1).wait_recv()
                ring_d[h, s] = (
                    ring_d[h, s].astype(jnp.float32) + chosen.astype(jnp.float32)
                ).astype(jnp.bfloat16)

            @pl.when(s < NZ - 1)
            def _(h=h):
                ring3_copy(h, s).start()
                ring_d_copy(h, s).start()

    quarter = width // 4

    def piece(xx, yy):
        i = xx * NY + yy
        return ring3.at[i // 8, NZ - 1, pl.ds(pl.multiple_of((i % 8) * 8, 8), 8)]

    def send_three_and_donors():
        recv_xy[0] = piece(x, y)[...]
        for dx, dy in XY_ORDER:
            spread(
                piece((x + dx) % NX, (y + dy) % NY), recv_xy.at[dx * NY + dy], sem_xy,
                wide_peer((dx, dy, 0)),
            ).start()
        for h in range(2):
            rows_d[h] = ring_d[h, NZ - 1].astype(jnp.float32)

        def lay(k, _):
            to = wide_index(offset(k)) // NC
            for h in range(2):
                for j in range(4):
                    send_d[k, 4 * h + j : 4 * h + j + 1, :] = rows_d[
                        h, pl.ds(to, 1), j * quarter : (j + 1) * quarter
                    ]
            return 0

        lax.fori_loop(0, NX * NY, lay, 0)
        recv_d[0] = send_d[0]
        for dx, dy in XY_ORDER:
            k = dx * NY + dy
            spread(send_d.at[k], recv_d.at[k], sem_d, wide_peer((dx, dy, 0))).start()

    def join_three_and_donors():
        join_xy(recv_xy, sem_xy)
        total = recv_xy[0]
        for k in range(1, NX * NY):
            total = total + recv_xy[k]
        recv_three[0] = total
        join_xy(recv_d, sem_d)
        total = recv_d[0]
        for k in range(1, NX * NY):
            total = total + recv_d[k]
        final_d[...] = total

    def finish_three():
        join_xy(recv_three, sem_three)
        to_core(recv_three, sem_three_c).start()
        to_core(recv_three, sem_three_c).wait()

        def lay(k, _):
            src = source_of(k)
            i = src // 2
            row = (src % 2) * mine + (i % 8) * 8
            three[i // 8, pl.ds(pl.multiple_of(row, 8), 8), :] = recv_three[k]
            return 0

        lax.fori_loop(0, NW, lay, 0)
        masses = totals[:, 2 * devices : 2 * devices + per_z]
        mass_row = jnp.sum(
            jnp.where(iota((8, per_z), 0) == z, masses, 0.0), axis=0, keepdims=True
        )
        diagonal = iota((per_z, per_z), 0) == iota((per_z, per_z), 1)
        mass = jnp.sum(jnp.where(diagonal, mass_row, 0.0), axis=1, keepdims=True)
        mass = jnp.maximum(mass, 1.0)
        chosen = par3[...] == iota((8, per_z), 0) + 8 * w
        pick = chosen.astype(jnp.float32).astype(jnp.bfloat16)
        for h in range(2):
            out3[:, h * half : (h + 1) * half] = three[h] / mass
            total = jnp.zeros((8, half), jnp.float32)
            for term in three_terms(three[h]):
                total = total + jnp.dot(pick, term, preferred_element_type=jnp.float32)
            recv_four[0, :, h * half : (h + 1) * half] = total
        mass_four = jnp.sum(jnp.where(chosen, mass_row, 0.0), axis=1, keepdims=True)
        recv_four[0, :, width : width + 128] = jnp.broadcast_to(mass_four, (8, 128))
        spread_z(recv_four.at[0], recv_four, sem_four)

    def send_four():
        join_z(recv_four, sem_four)
        acc_four[...] = recv_four[z]
        for zz in range(1, NZ):
            acc_four[...] += recv_four[(z + NZ - zz) % NZ]
        mass = jnp.maximum(acc_four[:, width : width + 1], 1.0)
        recv_out[0] = acc_four[:, 0:width] / mass
        spread_xy(recv_out.at[0], recv_out, sem_out)

    def finish_four():
        to_core(recv_out, sem_out_c).wait()

        def lay(k, _):
            out4[pl.ds(pl.multiple_of(source_of(k) * 8, 8), 8), :] = recv_out[k]
            return 0

        lax.fori_loop(0, NW, lay, 0)

    def q_copy(h, t):
        return pltpu.make_async_remote_copy(
            src_ref=ring_q.at[h, t], dst_ref=ring_q.at[h, t + 1],
            send_sem=q_send.at[h, t], recv_sem=q_recv.at[h, t + 1],
            device_id=z_peer((1, NZ - 1)[h]), device_id_type=MESH,
        )

    def s_copy(h, t):
        return pltpu.make_async_remote_copy(
            src_ref=ring_s.at[h, t], dst_ref=ring_s.at[h, t + 1],
            send_sem=sc_send.at[h, t], recv_sem=sc_recv.at[h, t + 1],
            device_id=z_peer((1, NZ - 1)[h]), device_id_type=MESH,
        )

    groups = half // 128

    def take_in(h, t):
        q_copy(h, t - 1).wait_recv()
        s_copy(h, t - 1).wait_recv()
        turn[0:8, :] = ring_s[h, t]
        scale = jnp.transpose(turn[...]) * (1.0 / TOP)
        for j in range(groups):
            at = slice(j * 128, (j + 1) * 128)
            value = ring_q[h, t, :, at].astype(jnp.int32).astype(jnp.float32)
            acc[h, :, at] += value * scale[:, j : j + 1]

    def pass_on(h, t):
        scale = jnp.zeros((clusters, 128), jnp.float32)
        for j in range(groups):
            at = slice(j * 128, (j + 1) * 128)
            value = acc[h, :, at]
            top = jnp.maximum(jnp.max(jnp.abs(value), axis=1, keepdims=True), 1e-37)
            scale = jnp.where(iota((clusters, 128), 1) == j, top, scale)
            ring_q[h, t, :, at] = (
                jnp.round(value * (1.0 / top) * TOP).astype(jnp.int32).astype(jnp.int16)
            )
        ring_s[h, t] = jnp.transpose(scale)[0:8, :]
        q_copy(h, t).start()
        s_copy(h, t).start()

    def reduce_stage(t):
        all_wide(sbuf.at[0], rbuf.at[t], s_sem.at[0], r_sem.at[t]).wait_recv()
        for h, blk in enumerate((block_f(t), block_b(t))):
            hit, counts = matched(blk)
            assign = jnp.where(hit, counts, 0.0).astype(jnp.bfloat16)
            for n in range(half // tile):
                acc[h, :, n * tile : (n + 1) * tile] = jnp.dot(
                    assign,
                    rbuf[t, :, h * half + n * tile : h * half + (n + 1) * tile],
                    preferred_element_type=jnp.float32,
                )
        for h in range(2):
            pl.when(t > 0)(lambda h=h: take_in(h, t))
            pl.when(t < NZ - 1)(lambda h=h: pass_on(h, t))

    def at_stage(t, which, work):
        pl.when(t == which)(work)

    def stage(t, _):
        @pl.when(t < NZ - 1)
        def _():
            pack(t + 1)

        at_stage(t, 0, reduce_weights_z)

        @pl.when((t >= 1) & (t <= 4))
        def _():
            step_three(2 * t - 1)

        at_stage(t, 4, send_three_and_donors)
        at_stage(t, 5, lambda: spread_xy(recv_three.at[0], recv_three, sem_three))
        at_stage(t, 6, send_four)

        @pl.when(t < NZ - 1)
        def _():
            send(t + 1)

        reduce_stage(t)

        @pl.when(t == 0)
        def _():
            reduce_weights_wide()
            pick_donors()
            local_three(0)
            spread(donors_c, donors_c, sem_donors_c, wide_peer((0, 0, 1))).wait()

        @pl.when(t <= 3)
        def _():
            step_three(2 * t)

        at_stage(t, 4, join_three_and_donors)
        at_stage(t, 5, finish_three)

        @pl.when(t == 6)
        def _():
            join_xy(recv_out, sem_out)
            to_core(recv_out, sem_out_c).start()

        return 0

    lax.fori_loop(0, NZ, stage, 0)

    others = pl.ds(1, NZ - 1)
    spread(w_send.at[others], w_recv.at[others], sem_w, z_peer(1)).wait()
    total = w_send[0]
    for k in range(1, NZ):
        total = total + w_recv[k]
    diagonal = iota((clusters, clusters), 0) == iota((clusters, clusters), 1)
    mass = jnp.sum(jnp.where(diagonal, total[0:1, :], 0.0), axis=1, keepdims=True)
    mass = jnp.maximum(mass, 1.0)
    seeded = [iota((clusters, 1), 0) == reseed[0:1, k : k + 1] for k in range(2)]
    for j in range(4):
        at = (j % 2) * quarter
        value = acc[j // 2, :, at : at + quarter] / mass
        for k in range(2):
            value = jnp.where(seeded[k], final_d[4 * k + j : 4 * k + j + 1, :], value)
        out2[:, j * quarter : (j + 1) * quarter] = value

    finish_four()
    for b in range(SEND_BUFFERS):
        all_wide(sbuf.at[b], rbuf.at[0], s_sem.at[b], r_sem.at[0]).wait_send()
    for b in range(2):
        core_copy(b).wait_send()

    def drain(t, _):
        for h in range(2):
            q_copy(h, t).wait_send()
            s_copy(h, t).wait_send()
            ring3_copy(h, t).wait_send()
            ring_d_copy(h, t).wait_send()
        return 0

    lax.fori_loop(0, NZ - 1, drain, 0)


def per_device(
    embeddings,
    point_counts,
    owner_ids,
    owner_slots,
    reseed_slots,
    donor_ids,
    parents_two,
    parents_three,
):
    rows, width = embeddings.shape
    clusters = parents_two.shape[0]
    per_z = parents_three.shape[0]
    half = width // 2
    places = NW * CAP
    devices = NW * NZ
    f32, bf16 = jnp.float32, jnp.bfloat16
    vmem = pl.BlockSpec(memory_space=pltpu.VMEM)
    dma = pltpu.SemaphoreType.DMA
    return pl.pallas_call(
        centroid_kernel,
        out_shape=(
            jax.ShapeDtypeStruct((clusters, width), f32),
            jax.ShapeDtypeStruct((per_z, width), f32),
            jax.ShapeDtypeStruct((L4, width), f32),
        ),
        in_specs=[pl.BlockSpec(memory_space=pl.ANY)] + [vmem] * 7,
        out_specs=(vmem,) * 3,
        scratch_shapes=[
            pltpu.VMEM((rows, width), bf16),
            pltpu.VMEM((SEND_BUFFERS, places, width), bf16),
            pltpu.VMEM((NZ, places, width), bf16),
            pltpu.VMEM((places, rows), bf16),
            pltpu.VMEM((8, rows), jnp.int32),
            pltpu.VMEM((places, 128), bf16),
            pltpu.VMEM((places, 128), bf16),
            pltpu.VMEM((16, places), f32),
            pltpu.VMEM((2, NZ, clusters, half), jnp.int16),
            pltpu.VMEM((2, NZ, 8, clusters), f32),
            pltpu.VMEM((2, clusters, half), f32),
            pltpu.VMEM((128, clusters), f32),
            pltpu.VMEM((NZ, 8, clusters), f32),
            pltpu.VMEM((NZ, 8, clusters), f32),
            pltpu.VMEM((NZ, NZ, clusters + 128), f32),
            pltpu.VMEM((NW, NZ, clusters + 128), f32),
            pltpu.VMEM((devices, clusters), f32),
            pltpu.VMEM((devices, 128), f32),
            pltpu.VMEM((NZ, 8, 128 + per_z), f32),
            pltpu.VMEM((NX * NY, 8, 128 + per_z), f32),
            pltpu.VMEM((2, 8, 128 + per_z), jnp.int32),
            pltpu.VMEM((8, 2 * devices + per_z), f32),
            pltpu.VMEM((2 * devices, width), bf16),
            pltpu.VMEM((2, devices // NC, width), bf16),
            pltpu.VMEM((2, 2, per_z, half), f32),
            pltpu.VMEM((2, 2, per_z // NC, half), f32),
            pltpu.VMEM((NZ, 2, per_z // NC, half), f32),
            pltpu.VMEM((2, NZ, per_z // NC, half), f32),
            pltpu.VMEM((2, NZ, NX * NY, width), bf16),
            pltpu.VMEM((2, NX * NY, width), f32),
            pltpu.VMEM((NX * NY, 8, width // 4), f32),
            pltpu.VMEM((NX * NY, 8, width // 4), f32),
            pltpu.VMEM((8, width // 4), f32),
            pltpu.VMEM((NX * NY, 8, half), f32),
            pltpu.VMEM((NW, 8, half), f32),
            pltpu.VMEM((2, per_z, half), f32),
            pltpu.VMEM((NZ, 8, width + 128), f32),
            pltpu.VMEM((NW, 8, width), f32),
            pltpu.VMEM((8, width + 128), f32),
            dma((1,)),
            dma((SEND_BUFFERS,)),
            dma((NZ,)),
            dma((2, NZ)),
            dma((2, NZ)),
            dma((2, NZ)),
            dma((2, NZ)),
            dma((16, 2)),
            dma((2,)),
            dma((NZ,)),
            dma((2, NZ)),
            dma((2, NZ)),
            dma((2, NZ)),
            dma((2, NZ)),
        ],
        compiler_params=pltpu.CompilerParams(
            collective_id=0, has_side_effects=True, vmem_limit_bytes=63 * 2**20
        ),
    )(
        embeddings,
        owner_ids.reshape(1, rows),
        owner_slots.reshape(1, rows),
        point_counts.reshape(1, rows),
        parents_two.reshape(1, clusters),
        parents_three.reshape(1, per_z),
        reseed_slots,
        donor_ids,
    )


def solution(mesh):
    in_specs = (
        P(("wide", "narrow"), None),
        P(("wide", "narrow")),
        P(("wide", "narrow"), None),
        P(("wide", "narrow"), None),
        P(("wide", "narrow"), None),
        P(("wide", "narrow"), None),
        P(("wide", "narrow")),
        P("narrow"),
    )
    out_specs = (P(("wide", "narrow"), None), P("narrow", None), P())
    return jax.shard_map(
        per_device, mesh=mesh, in_specs=in_specs, out_specs=out_specs, check_vma=False
    )
```

```python
import jax
import jax.numpy as jnp
from jax import lax
from jax.experimental import pallas as pl
from jax.experimental.pallas import tpu as pltpu
from jax.sharding import PartitionSpec as P

L4 = 256
CAP = 16
NX, NY, NC, NZ = 4, 4, 2, 8
NW = NX * NY * NC
MESH = pl.DeviceIdType.MESH
TOP = 32767.0
SEND_BUFFERS = 3

XY_ORDER = [
    (1, 0), (0, 1), (3, 0), (0, 3), (2, 2), (1, 1), (3, 3), (1, 3),
    (3, 1), (2, 0), (0, 2), (2, 1), (1, 2), (2, 3), (3, 2),
]
WIDE_ORDER = [(dx, dy, dc) for dc in range(NC) for dx, dy in XY_ORDER] + [(0, 0, 1)]


def rel_of(d):
    return (d[2] * NX + d[0]) * NY + d[1]


def nt_dot(a, b):
    return lax.dot_general(
        a, b, (((1,), (1,)), ((), ())), preferred_element_type=jnp.float32
    )


def iota(shape, axis):
    return lax.broadcasted_iota(jnp.int32, shape, axis)


def centroid_kernel(
    emb_hbm, own, slot, cnt, par2, par3, reseed, donor,
    out2, out3, out4,
    emb, sbuf, rbuf, onehot, pos, lab_send, lab_recv, lab_t, ring_q, ring_s, acc, turn, mass_two, w_send, w_recv,
    info_z, info_w, tab, req, red_z, red_w, red_c, totals, picked, donors_c,
    part, core_send, core_recv, three_q, three_s, acc3, turn3, ring_d, rows_d, send_d, recv_d, final_d,
    recv_xy, recv_three, three, recv_four, recv_out, acc_four,
    load_sem, s_sem, r_sem, q_send, q_recv, sc_send, sc_recv, once, core_s, core_r, s3_sem, r3_sem, sc3_send, sc3_recv,
    sd_sem, rd_sem,
):
    load = pltpu.make_async_copy(emb_hbm, emb, load_sem.at[0])
    load.start()
    rows, width = emb.shape
    half = width // 2
    clusters = out2.shape[0]
    per_z = out3.shape[0]
    mine = per_z // NC
    w = lax.axis_index("wide")
    z = lax.axis_index("narrow")
    x, y, c = w // 8, (w // 2) % 4, w % 2

    def wide_index(d):
        return ((x + d[0]) % NX) * 8 + ((y + d[1]) % NY) * 2 + (c + d[2]) % NC

    def wide_peer(d):
        return (wide_index(d), z)

    def offset(k):
        return (k // NY) % NX, k % NY, k // (NX * NY)

    def source_of(k):
        dx, dy, dc = offset(k)
        return wide_index((NX - dx, NY - dy, dc))

    def z_peer(k):
        return (w, (z + k) % NZ)

    barrier = pltpu.get_barrier_semaphore()
    for d in WIDE_ORDER:
        pl.semaphore_signal(barrier, inc=1, device_id=wide_peer(d), device_id_type=MESH)
    for k in range(1, NZ):
        pl.semaphore_signal(barrier, inc=1, device_id=z_peer(k), device_id_type=MESH)

    def spread(src, dst, sems, device):
        return pltpu.make_async_remote_copy(
            src_ref=src, dst_ref=dst, send_sem=sems.at[0], recv_sem=sems.at[1],
            device_id=device, device_id_type=MESH,
        )

    def spread_z(src, dst, sems):
        for k in range(1, NZ):
            spread(src, dst.at[k], sems, z_peer(k)).start()

    def join_z(dst, sems):
        at = pl.ds(1, NZ - 1)
        spread(dst.at[at], dst.at[at], sems, z_peer(1)).wait()

    def spread_xy(src, dst, sems):
        for dx, dy in XY_ORDER:
            spread(src, dst.at[dx * NY + dy], sems, wide_peer((dx, dy, 0))).start()

    def join_xy(dst, sems):
        at = pl.ds(1, NX * NY - 1)
        spread(dst.at[at], dst.at[at], sems, wide_peer((0, 1, 0))).wait()

    def to_core(dst, sems):
        here, there = pl.ds(0, NX * NY), pl.ds(NX * NY, NX * NY)
        return spread(dst.at[here], dst.at[there], sems, wide_peer((0, 0, 1)))

    sem_info_z, sem_info_w, sem_lab, sem_w = once.at[0], once.at[1], once.at[2], once.at[3]
    sem_red_z, sem_red_w, sem_xy, sem_d = once.at[4], once.at[5], once.at[6], once.at[7]
    sem_three, sem_four, sem_out = once.at[8], once.at[9], once.at[10]
    sem_info_c, sem_red_c, sem_three_c = once.at[11], once.at[12], once.at[13]
    sem_out_c, sem_donors_c = once.at[14], once.at[15]

    slots = iota((1, clusters), 1)
    parent = par2[...].astype(jnp.float32)
    hits = [slots == reseed[0:1, k : k + 1] for k in range(2)]
    grands = [jnp.sum(jnp.where(h, parent, 0.0), axis=1, keepdims=True) for h in hits]
    table = parent + jnp.where(hits[0] | hits[1], 1024.0, 0.0)
    lane = iota((1, 128), 1)
    extra = jnp.zeros((1, 128), jnp.float32)
    for i, v in enumerate(
        [donor[0:1, 0:1], donor[0:1, 1:2], grands[0], grands[1], reseed[0:1, 0:1], reseed[0:1, 1:2]]
    ):
        extra = jnp.where(lane == i, v.astype(jnp.float32), extra)
    info_z[0, :, 0:clusters] = jnp.where(iota((NZ, clusters), 0) == z, table, 0.0)
    info_z[0, :, clusters : clusters + 128] = jnp.where(iota((NZ, 128), 0) == z, extra, 0.0)

    pl.semaphore_wait(barrier, NW - 1 + NZ - 1)
    spread_z(info_z.at[0], info_z, sem_info_z)

    owner = own[...]
    target = owner // NZ
    rel = (
        ((target - c) & 1) * 16 + ((target // 8 - x) & 3) * 4 + (((target // 2) - y) & 3)
    )
    step = 256
    upper = (iota((step, step), 0) < iota((step, step), 1)).astype(jnp.bfloat16)
    carry = jnp.zeros((step, 1), jnp.float32)
    for b in range(rows // step):
        cols = slice(b * step, (b + 1) * step)
        hit = iota((step, step), 0) == owner[:, cols]
        mark = hit.astype(jnp.bfloat16)
        earlier = jnp.dot(mark, upper, preferred_element_type=jnp.float32) + carry
        mark32 = hit.astype(jnp.float32)
        rank = jnp.sum(earlier * mark32, axis=0, keepdims=True)
        carry = carry + jnp.sum(mark32, axis=1, keepdims=True)
        pos[0:1, cols] = rel[:, cols] * CAP + rank.astype(jnp.int32)
    pos[1:2, :] = owner % NZ


    places = NW * CAP
    tile = 256

    def fill_onehot(where_row):
        for i in range(places // tile):
            ids = iota((tile, rows), 0) + i * tile
            onehot[i * tile : (i + 1) * tile, :] = (ids == where_row).astype(jnp.bfloat16)

    def send_wide(src, dst, sem_s, sem_r):
        for d in WIDE_ORDER:
            at = pl.ds(rel_of(d) * CAP, CAP)
            pltpu.make_async_remote_copy(
                src_ref=src.at[at], dst_ref=dst.at[at], send_sem=sem_s, recv_sem=sem_r,
                device_id=wide_peer(d), device_id_type=MESH,
            ).start()

    def all_wide(src, dst, sem_s, sem_r):
        at = pl.ds(CAP, places - CAP)
        return pltpu.make_async_remote_copy(
            src_ref=src.at[at], dst_ref=dst.at[at], send_sem=sem_s, recv_sem=sem_r,
            device_id=wide_peer((0, 0, 1)), device_id_type=MESH,
        )


    def block_f(t):
        return (z + 2 * NZ - 1 - t) % NZ

    def block_b(t):
        return (z + 1 + t) % NZ

    def pack_half(t, h):
        b = lax.rem(t, SEND_BUFFERS)
        blk = (block_f, block_b)[h](t)
        fill_onehot(jnp.where(pos[1:2, :] == blk, pos[0:1, :], -1))

        def column(n, _):
            at = pl.ds(pl.multiple_of(h * half + n * tile, tile), tile)
            sbuf[b, :, at] = jnp.dot(
                onehot[...], emb[:, at], preferred_element_type=jnp.float32
            ).astype(jnp.bfloat16)
            return 0

        lax.fori_loop(0, half // tile, column, 0)

    def pack(t):
        b = lax.rem(t, SEND_BUFFERS)

        @pl.when(t >= SEND_BUFFERS)
        def _():
            all_wide(sbuf.at[b], rbuf.at[t], s_sem.at[b], r_sem.at[t]).wait_send()

        for h in range(2):
            pack_half(t, h)
        rbuf[t, 0:CAP, :] = sbuf[b, 0:CAP, :]

    def send(t):
        b = lax.rem(t, SEND_BUFFERS)
        send_wide(sbuf.at[b], rbuf.at[t], s_sem.at[b], r_sem.at[t])

    join_z(info_z, sem_info_z)
    whole = info_z[0]
    for k in range(1, NZ):
        whole = whole + info_z[k]
    info_w[0] = whole
    spread_xy(info_w.at[0], info_w, sem_info_w)
    load.wait()
    pack_half(0, 0)
    join_xy(info_w, sem_info_w)
    to_core(info_w, sem_info_c).start()
    pack_half(0, 1)
    rbuf[0, 0:CAP, :] = sbuf[0, 0:CAP, :]
    send(0)

    turn[...] = jnp.zeros(turn.shape, jnp.float32)
    turn3[...] = jnp.zeros(turn3.shape, jnp.float32)

    def turn_labels():
        all_wide(lab_send, lab_recv, sem_lab.at[0], sem_lab.at[1]).wait()
        eye = (iota((16, 128), 0) == iota((16, 128), 1)).astype(jnp.bfloat16)
        lab_t[...] = nt_dot(eye, lab_recv[...])

    def matched(blk):
        ids = iota((clusters, places), 0).astype(jnp.float32)
        return ids == lab_t[pl.ds(2 * blk, 1), :], lab_t[pl.ds(2 * blk + 1, 1), :]

    def weigh(k, _):
        hit, counts = matched((z + k) % NZ)
        counts = jnp.broadcast_to(counts, (8, places)).astype(jnp.bfloat16)
        w_send[k] = nt_dot(counts, hit.astype(jnp.float32).astype(jnp.bfloat16))
        return 0

    def send_masses():
        lax.fori_loop(0, NZ, weigh, 0)
        for k in range(1, NZ):
            spread(w_send.at[k], w_recv.at[k], sem_w, z_peer(k)).start()

    def join_masses():
        others = pl.ds(1, NZ - 1)
        spread(w_send.at[others], w_recv.at[others], sem_w, z_peer(1)).wait()
        total = w_send[0]
        for k in range(1, NZ):
            total = total + w_recv[k]
        diagonal = iota((clusters, clusters), 0) == iota((clusters, clusters), 1)
        mass = jnp.sum(jnp.where(diagonal, total[0:1, :], 0.0), axis=1, keepdims=True)
        mass_two[...] = jnp.broadcast_to(jnp.maximum(mass, 1.0), mass_two.shape)

    to_core(info_w, sem_info_c).wait()

    devices = NW * NZ

    def arrange(k, _):
        src = source_of(k)
        tab[pl.ds(pl.multiple_of(src * NZ, NZ), NZ), :] = info_w[k, :, 0:clusters]
        for zz in range(NZ):
            row = (src % 2) * (devices // NC) + zz * (NX * NY) + src // 2
            req[pl.ds(row, 1), :] = info_w[k, zz : zz + 1, clusters : clusters + 128]
        return 0

    lax.fori_loop(0, NW, arrange, 0)
    across = jnp.transpose(tab[...])
    high = jnp.floor(across * (1.0 / 64.0))
    low = (across - 64.0 * high).astype(jnp.bfloat16)
    high = high.astype(jnp.bfloat16)
    for b in range(rows // step):
        cols = slice(b * step, (b + 1) * step)
        mark = (iota((step, step), 0) == own[:, cols]).astype(jnp.bfloat16)
        values = 64.0 * jnp.dot(high, mark, preferred_element_type=jnp.float32) + jnp.dot(
            low, mark, preferred_element_type=jnp.float32
        )
        found = jnp.sum(
            jnp.where(iota((clusters, step), 0) == slot[:, cols], values, 0.0),
            axis=0, keepdims=True,
        ).astype(jnp.int32)
        gone = found >= 1024
        true_parent = jnp.where(gone, found - 1024, found)
        pos[2:3, cols] = jnp.where(gone, -1, true_parent)
        pos[3:4, cols] = true_parent

    place = iota((devices, 1), 0)
    owner_of = ((place % 16) * NC + place // 128) * NZ + (place // 16) % NZ
    ident = own[...] * clusters + slot[...]
    for k in range(2):
        asked = owner_of * clusters + req[:, 4 + k : 5 + k].astype(jnp.int32)
        onehot[k * devices : (k + 1) * devices, :] = (asked == ident).astype(jnp.bfloat16)
    counts32 = cnt[...].astype(jnp.float32)
    counts8 = jnp.broadcast_to(counts32, (8, rows)).astype(jnp.bfloat16)
    true_parent = pos[3:4, :]
    by_z = jnp.where(iota((8, rows), 0) == true_parent // per_z, counts32, 0.0).astype(jnp.bfloat16)
    inside = (iota((per_z, rows), 0) == true_parent % per_z).astype(jnp.bfloat16)
    asked_weights = nt_dot(counts8, onehot[...])
    folded = jnp.zeros((8, 128), jnp.float32)
    for i in range(2 * devices // 128):
        folded = jnp.where(
            iota((8, 128), 0) == i, asked_weights[:, i * 128 : (i + 1) * 128], folded
        )
    red_z[0, :, 0:128] = folded
    red_z[0, :, 128 : 128 + per_z] = nt_dot(by_z, inside)
    spread_z(red_z.at[0], red_z, sem_red_z)

    fill_onehot(pos[0:1, :])
    deep = iota((128, rows), 0)
    z_of = pos[1:2, :]
    labels = jnp.where(
        deep == 2 * z_of, slot[...], jnp.where(deep == 2 * z_of + 1, cnt[...], 0)
    ).astype(jnp.float32).astype(jnp.bfloat16)
    lab_send[...] = nt_dot(onehot[...], labels).astype(jnp.bfloat16)
    lab_recv[0:CAP, :] = lab_send[0:CAP, :]
    send_wide(lab_send, lab_recv, sem_lab.at[0], sem_lab.at[1])

    def reduce_weights_z():
        join_z(red_z, sem_red_z)
        total = red_z[0]
        for k in range(1, NZ):
            total = total + red_z[k]
        red_w[0] = total
        spread_xy(red_w.at[0], red_w, sem_red_w)

    def reduce_weights_wide():
        join_xy(red_w, sem_red_w)
        total = red_w[0].astype(jnp.int32)
        for k in range(1, NX * NY):
            total = total + red_w[k].astype(jnp.int32)
        red_c[0] = total
        swap = spread(red_c.at[0], red_c.at[1], sem_red_c, wide_peer((0, 0, 1)))
        swap.start()
        swap.wait()
        total = (total + red_c[1]).astype(jnp.float32)
        for i in range(2 * devices // 128):
            totals[0:1, i * 128 : (i + 1) * 128] = total[i : i + 1, 0:128]
        totals[:, 2 * devices : 2 * devices + per_z] = total[:, 128 : 128 + per_z]

    def pick_donors():
        first = (w * NZ + z) * rows
        for k in range(2):
            local = req[:, k : k + 1].astype(jnp.int32) - first
            onehot[k * devices : (k + 1) * devices, :] = (
                iota((devices, rows), 1) == local
            ).astype(jnp.bfloat16)

        def column(n, _):
            at = pl.ds(pl.multiple_of(n * tile, tile), tile)
            picked[:, at] = jnp.dot(
                onehot[...], emb[:, at], preferred_element_type=jnp.float32
            ).astype(jnp.bfloat16)
            return 0

        lax.fori_loop(0, width // tile, column, 0)
        for k in range(2):
            donors_copy(k).start()

    def donors_copy(k):
        at = pl.ds(pl.multiple_of(k * devices + (1 - c) * 128, 128), 128)
        return spread(picked.at[at], donors_c.at[k], sem_donors_c, wide_peer((0, 0, 1)))

    def core_copy(s):
        b = lax.rem(s, 2)
        return pltpu.make_async_remote_copy(
            src_ref=core_send.at[b], dst_ref=core_recv.at[s],
            send_sem=core_s.at[b], recv_sem=core_r.at[s],
            device_id=wide_peer((0, 0, 1)), device_id_type=MESH,
        )

    def three_terms(value):
        first = value.astype(jnp.bfloat16)
        rest = value - first.astype(jnp.float32)
        second = rest.astype(jnp.bfloat16)
        return first, second, (rest - second.astype(jnp.float32)).astype(jnp.bfloat16)

    def local_three(s):
        b = lax.rem(s, 2)

        @pl.when(s >= 2)
        def _():
            core_copy(s - 2).wait_send()

        grand_rows = jnp.transpose(req[...])
        for h, blk in enumerate((block_f(s), block_b(s))):
            base = jnp.where(
                iota((per_z, rows), 0) + per_z * blk == pos[2:3, :], cnt[...], 0
            ).astype(jnp.float32).astype(jnp.bfloat16)
            ids = (iota((per_z, devices), 0) + per_z * blk).astype(jnp.float32)
            heavy = [
                three_terms(
                    jnp.where(
                        ids == grand_rows[2 + k : 3 + k, :],
                        totals[0:1, k * devices : (k + 1) * devices],
                        0.0,
                    )
                )
                for k in range(2)
            ]
            for n in range(half // tile):
                at = slice(h * half + n * tile, h * half + (n + 1) * tile)
                value = jnp.dot(base, emb[:, at], preferred_element_type=jnp.float32)
                for k in range(2):
                    for term in heavy[k]:
                        value = value + jnp.dot(
                            term,
                            picked[k * devices : (k + 1) * devices, at],
                            preferred_element_type=jnp.float32,
                        )
                part[b, h, :, n * tile : (n + 1) * tile] = value
            core_send[b, h] = part[b, h, pl.ds(pl.multiple_of((1 - c) * mine, mine), mine), :]
        core_copy(s).start()

    groups = half // 128

    def fixed_ring(q, sc, total, turned, q_sems, sc_sems):
        rows_in, lanes = total.shape[1], turned.shape[1]

        def copies(h, t):
            to = z_peer((1, NZ - 1)[h])
            return [
                pltpu.make_async_remote_copy(
                    src_ref=ref.at[h, t], dst_ref=ref.at[h, t + 1],
                    send_sem=sems[0].at[h, t], recv_sem=sems[1].at[h, t + 1],
                    device_id=to, device_id_type=MESH,
                )
                for ref, sems in ((q, q_sems), (sc, sc_sems))
            ]

        def take_in(h, t):
            for copy in copies(h, t - 1):
                copy.wait_recv()
            turned[0:8, :] = sc[h, t]
            scale = jnp.transpose(turned[...])[0:rows_in, :] * (1.0 / TOP)
            for j in range(groups):
                at = slice(j * 128, (j + 1) * 128)
                value = q[h, t, :, at].astype(jnp.int32).astype(jnp.float32)
                total[h, :, at] += value * scale[:, j : j + 1]

        def pass_on(h, t):
            scale = jnp.zeros((rows_in, 128), jnp.float32)
            for j in range(groups):
                at = slice(j * 128, (j + 1) * 128)
                value = total[h, :, at]
                top = jnp.maximum(jnp.max(jnp.abs(value), axis=1, keepdims=True), 1e-37)
                scale = jnp.where(iota((rows_in, 128), 1) == j, top, scale)
                q[h, t, :, at] = (
                    jnp.round(value * (1.0 / top) * TOP).astype(jnp.int32).astype(jnp.int16)
                )
            if rows_in < lanes:
                filler = jnp.zeros((lanes - rows_in, 128), jnp.float32)
                scale = jnp.concatenate([scale, filler], axis=0)
            sc[h, t] = jnp.transpose(scale)[0:8, :]
            for copy in copies(h, t):
                copy.start()

        def drain(h, t):
            for copy in copies(h, t):
                copy.wait_send()

        return take_in, pass_on, drain

    take_in, pass_on, drain_two = fixed_ring(
        ring_q, ring_s, acc, turn, (q_send, q_recv), (sc_send, sc_recv)
    )
    take_three, pass_three, drain_three = fixed_ring(
        three_q, three_s, acc3, turn3, (s3_sem, r3_sem), (sc3_send, sc3_recv)
    )

    def ring_d_copy(h, s):
        return pltpu.make_async_remote_copy(
            src_ref=ring_d.at[h, s], dst_ref=ring_d.at[h, s + 1],
            send_sem=sd_sem.at[h, s], recv_sem=rd_sem.at[h, s + 1],
            device_id=z_peer((1, NZ - 1)[h]), device_id_type=MESH,
        )

    def step_three(s):
        @pl.when(s < NZ - 1)
        def _():
            local_three(s + 1)

        b = lax.rem(s, 2)
        core_copy(s).wait_recv()
        for h, blk in enumerate((block_f(s), block_b(s))):
            at = pl.ds(pl.multiple_of(c * mine, mine), mine)
            acc3[h] = part[b, h, at, :] + core_recv[s, h]
            at = pl.ds(pl.multiple_of(h * devices + c * 128 + blk * 16, 16), 16)
            chosen = (
                picked[at, :].astype(jnp.float32)
                + donors_c[h, pl.ds(pl.multiple_of(blk * 16, 16), 16), :].astype(jnp.float32)
            ).astype(jnp.bfloat16)

            @pl.when(s == 0)
            def _(h=h, chosen=chosen):
                ring_d[h, s] = chosen

            @pl.when(s > 0)
            def _(h=h, chosen=chosen):
                take_three(h, s)
                ring_d_copy(h, s - 1).wait_recv()
                ring_d[h, s] = (
                    ring_d[h, s].astype(jnp.float32) + chosen.astype(jnp.float32)
                ).astype(jnp.bfloat16)

            @pl.when(s < NZ - 1)
            def _(h=h):
                pass_three(h, s)
                ring_d_copy(h, s).start()

    quarter = width // 4

    def piece(xx, yy):
        i = xx * NY + yy
        return acc3.at[i // 8, pl.ds(pl.multiple_of((i % 8) * 8, 8), 8)]

    def send_three_and_donors():
        recv_xy[0] = piece(x, y)[...]
        for dx, dy in XY_ORDER:
            spread(
                piece((x + dx) % NX, (y + dy) % NY), recv_xy.at[dx * NY + dy], sem_xy,
                wide_peer((dx, dy, 0)),
            ).start()
        for h in range(2):
            rows_d[h] = ring_d[h, NZ - 1].astype(jnp.float32)

        def lay(k, _):
            to = wide_index(offset(k)) // NC
            for h in range(2):
                for j in range(4):
                    send_d[k, 4 * h + j : 4 * h + j + 1, :] = rows_d[
                        h, pl.ds(to, 1), j * quarter : (j + 1) * quarter
                    ]
            return 0

        lax.fori_loop(0, NX * NY, lay, 0)
        recv_d[0] = send_d[0]
        for dx, dy in XY_ORDER:
            k = dx * NY + dy
            spread(send_d.at[k], recv_d.at[k], sem_d, wide_peer((dx, dy, 0))).start()

    def join_three_and_donors():
        join_xy(recv_xy, sem_xy)
        total = recv_xy[0]
        for k in range(1, NX * NY):
            total = total + recv_xy[k]
        recv_three[0] = total
        join_xy(recv_d, sem_d)
        total = recv_d[0]
        for k in range(1, NX * NY):
            total = total + recv_d[k]
        final_d[...] = total

    def finish_three():
        join_xy(recv_three, sem_three)
        to_core(recv_three, sem_three_c).start()
        to_core(recv_three, sem_three_c).wait()

        def lay(k, _):
            src = source_of(k)
            i = src // 2
            row = (src % 2) * mine + (i % 8) * 8
            three[i // 8, pl.ds(pl.multiple_of(row, 8), 8), :] = recv_three[k]
            return 0

        lax.fori_loop(0, NW, lay, 0)
        masses = totals[:, 2 * devices : 2 * devices + per_z]
        mass_row = jnp.sum(
            jnp.where(iota((8, per_z), 0) == z, masses, 0.0), axis=0, keepdims=True
        )
        diagonal = iota((per_z, per_z), 0) == iota((per_z, per_z), 1)
        mass = jnp.sum(jnp.where(diagonal, mass_row, 0.0), axis=1, keepdims=True)
        mass = jnp.maximum(mass, 1.0)
        chosen = par3[...] == iota((8, per_z), 0) + 8 * w
        pick = chosen.astype(jnp.float32).astype(jnp.bfloat16)
        for h in range(2):
            out3[:, h * half : (h + 1) * half] = three[h] / mass
            total = jnp.zeros((8, half), jnp.float32)
            for term in three_terms(three[h]):
                total = total + jnp.dot(pick, term, preferred_element_type=jnp.float32)
            recv_four[0, :, h * half : (h + 1) * half] = total
        mass_four = jnp.sum(jnp.where(chosen, mass_row, 0.0), axis=1, keepdims=True)
        recv_four[0, :, width : width + 128] = jnp.broadcast_to(mass_four, (8, 128))
        spread_z(recv_four.at[0], recv_four, sem_four)

    def send_four():
        join_z(recv_four, sem_four)
        acc_four[...] = recv_four[z]
        for zz in range(1, NZ):
            acc_four[...] += recv_four[(z + NZ - zz) % NZ]
        mass = jnp.maximum(acc_four[:, width : width + 1], 1.0)
        recv_out[0] = acc_four[:, 0:width] / mass
        spread_xy(recv_out.at[0], recv_out, sem_out)

    def finish_four():
        to_core(recv_out, sem_out_c).wait()

        def lay(k, _):
            out4[pl.ds(pl.multiple_of(source_of(k) * 8, 8), 8), :] = recv_out[k]
            return 0

        lax.fori_loop(0, NW, lay, 0)

    def reduce_stage(t):
        all_wide(sbuf.at[0], rbuf.at[t], s_sem.at[0], r_sem.at[t]).wait_recv()
        for h, blk in enumerate((block_f(t), block_b(t))):
            hit, counts = matched(blk)
            assign = jnp.where(hit, counts, 0.0).astype(jnp.bfloat16)
            for n in range(half // tile):
                acc[h, :, n * tile : (n + 1) * tile] = jnp.dot(
                    assign,
                    rbuf[t, :, h * half + n * tile : h * half + (n + 1) * tile],
                    preferred_element_type=jnp.float32,
                )
        for h in range(2):
            pl.when(t > 0)(lambda h=h: take_in(h, t))
            pl.when(t < NZ - 1)(lambda h=h: pass_on(h, t))

    def at_stage(t, which, work):
        pl.when(t == which)(work)

    def stage(t, _):
        @pl.when(t < NZ - 1)
        def _():
            pack(t + 1)

        at_stage(t, 0, reduce_weights_z)

        @pl.when(t == 4)
        def _():
            step_three(2 * t - 1)
            send_three_and_donors()

        at_stage(t, 5, lambda: spread_xy(recv_three.at[0], recv_three, sem_three))

        @pl.when(t < NZ - 1)
        def _():
            send(t + 1)

        @pl.when(t == 0)
        def _():
            pick_donors()
            turn_labels()

        at_stage(t, 1, send_masses)

        @pl.when((t >= 1) & (t <= 3))
        def _():
            step_three(2 * t - 1)

        at_stage(t, 6, send_four)
        at_stage(t, 7, join_masses)
        reduce_stage(t)

        @pl.when(t == 0)
        def _():
            reduce_weights_wide()
            local_three(0)
            spread(donors_c, donors_c, sem_donors_c, wide_peer((0, 0, 1))).wait()

        @pl.when(t <= 3)
        def _():
            step_three(2 * t)

        at_stage(t, 4, join_three_and_donors)
        at_stage(t, 5, finish_three)
        return 0

    lax.fori_loop(0, NZ, stage, 0)

    mass = mass_two[:, 0:1]
    seeded = [iota((clusters, 1), 0) == reseed[0:1, k : k + 1] for k in range(2)]
    for j in range(4):
        at = (j % 2) * quarter
        value = acc[j // 2, :, at : at + quarter] / mass
        for k in range(2):
            value = jnp.where(seeded[k], final_d[4 * k + j : 4 * k + j + 1, :], value)
        out2[:, j * quarter : (j + 1) * quarter] = value

    join_xy(recv_out, sem_out)
    to_core(recv_out, sem_out_c).start()
    finish_four()
    for b in range(SEND_BUFFERS):
        all_wide(sbuf.at[b], rbuf.at[0], s_sem.at[b], r_sem.at[0]).wait_send()
    for b in range(2):
        core_copy(b).wait_send()

    def drain(t, _):
        for h in range(2):
            drain_two(h, t)
            drain_three(h, t)
            ring_d_copy(h, t).wait_send()
        return 0

    lax.fori_loop(0, NZ - 1, drain, 0)


def per_device(
    embeddings,
    point_counts,
    owner_ids,
    owner_slots,
    reseed_slots,
    donor_ids,
    parents_two,
    parents_three,
):
    rows, width = embeddings.shape
    clusters = parents_two.shape[0]
    per_z = parents_three.shape[0]
    half = width // 2
    places = NW * CAP
    devices = NW * NZ
    f32, bf16 = jnp.float32, jnp.bfloat16
    vmem = pl.BlockSpec(memory_space=pltpu.VMEM)
    dma = pltpu.SemaphoreType.DMA
    return pl.pallas_call(
        centroid_kernel,
        out_shape=(
            jax.ShapeDtypeStruct((clusters, width), f32),
            jax.ShapeDtypeStruct((per_z, width), f32),
            jax.ShapeDtypeStruct((L4, width), f32),
        ),
        in_specs=[pl.BlockSpec(memory_space=pl.ANY)] + [vmem] * 7,
        out_specs=(vmem,) * 3,
        scratch_shapes=[
            pltpu.VMEM((rows, width), bf16),
            pltpu.VMEM((SEND_BUFFERS, places, width), bf16),
            pltpu.VMEM((NZ, places, width), bf16),
            pltpu.VMEM((places, rows), bf16),
            pltpu.VMEM((8, rows), jnp.int32),
            pltpu.VMEM((places, 128), bf16),
            pltpu.VMEM((places, 128), bf16),
            pltpu.VMEM((16, places), f32),
            pltpu.VMEM((2, NZ, clusters, half), jnp.int16),
            pltpu.VMEM((2, NZ, 8, clusters), f32),
            pltpu.VMEM((2, clusters, half), f32),
            pltpu.VMEM((128, clusters), f32),
            pltpu.VMEM((clusters, 128), f32),
            pltpu.VMEM((NZ, 8, clusters), f32),
            pltpu.VMEM((NZ, 8, clusters), f32),
            pltpu.VMEM((NZ, NZ, clusters + 128), f32),
            pltpu.VMEM((NW, NZ, clusters + 128), f32),
            pltpu.VMEM((devices, clusters), f32),
            pltpu.VMEM((devices, 128), f32),
            pltpu.VMEM((NZ, 8, 128 + per_z), f32),
            pltpu.VMEM((NX * NY, 8, 128 + per_z), f32),
            pltpu.VMEM((2, 8, 128 + per_z), jnp.int32),
            pltpu.VMEM((8, 2 * devices + per_z), f32),
            pltpu.VMEM((2 * devices, width), bf16),
            pltpu.VMEM((2, devices // NC, width), bf16),
            pltpu.VMEM((2, 2, per_z, half), f32),
            pltpu.VMEM((2, 2, per_z // NC, half), f32),
            pltpu.VMEM((NZ, 2, per_z // NC, half), f32),
            pltpu.VMEM((2, NZ, per_z // NC, half), jnp.int16),
            pltpu.VMEM((2, NZ, 8, 128), f32),
            pltpu.VMEM((2, per_z // NC, half), f32),
            pltpu.VMEM((128, 128), f32),
            pltpu.VMEM((2, NZ, NX * NY, width), bf16),
            pltpu.VMEM((2, NX * NY, width), f32),
            pltpu.VMEM((NX * NY, 8, width // 4), f32),
            pltpu.VMEM((NX * NY, 8, width // 4), f32),
            pltpu.VMEM((8, width // 4), f32),
            pltpu.VMEM((NX * NY, 8, half), f32),
            pltpu.VMEM((NW, 8, half), f32),
            pltpu.VMEM((2, per_z, half), f32),
            pltpu.VMEM((NZ, 8, width + 128), f32),
            pltpu.VMEM((NW, 8, width), f32),
            pltpu.VMEM((8, width + 128), f32),
            dma((1,)),
            dma((SEND_BUFFERS,)),
            dma((NZ,)),
            dma((2, NZ)),
            dma((2, NZ)),
            dma((2, NZ)),
            dma((2, NZ)),
            dma((16, 2)),
            dma((2,)),
            dma((NZ,)),
            dma((2, NZ)),
            dma((2, NZ)),
            dma((2, NZ)),
            dma((2, NZ)),
            dma((2, NZ)),
            dma((2, NZ)),
        ],
        compiler_params=pltpu.CompilerParams(
            collective_id=0, has_side_effects=True, vmem_limit_bytes=63 * 2**20
        ),
    )(
        embeddings,
        owner_ids.reshape(1, rows),
        owner_slots.reshape(1, rows),
        point_counts.reshape(1, rows),
        parents_two.reshape(1, clusters),
        parents_three.reshape(1, per_z),
        reseed_slots,
        donor_ids,
    )


def solution(mesh):
    in_specs = (
        P(("wide", "narrow"), None),
        P(("wide", "narrow")),
        P(("wide", "narrow"), None),
        P(("wide", "narrow"), None),
        P(("wide", "narrow"), None),
        P(("wide", "narrow"), None),
        P(("wide", "narrow")),
        P("narrow"),
    )
    out_specs = (P(("wide", "narrow"), None), P("narrow", None), P())
    return jax.shard_map(
        per_device, mesh=mesh, in_specs=in_specs, out_specs=out_specs, check_vma=False
    )
```

```python
import jax
import jax.numpy as jnp
from jax import lax
from jax.experimental import pallas as pl
from jax.experimental.pallas import tpu as pltpu
from jax.sharding import PartitionSpec as P

L4 = 256
CAP = 16
NX, NY, NC, NZ = 4, 4, 2, 8
NW = NX * NY * NC
MESH = pl.DeviceIdType.MESH
TOP = 32767.0
SEND_BUFFERS = 3

XY_ORDER = [
    (1, 0), (0, 1), (3, 0), (0, 3), (2, 2), (1, 1), (3, 3), (1, 3),
    (3, 1), (2, 0), (0, 2), (2, 1), (1, 2), (2, 3), (3, 2),
]
WIDE_ORDER = [(dx, dy, dc) for dc in range(NC) for dx, dy in XY_ORDER] + [(0, 0, 1)]


def rel_of(d):
    return (d[2] * NX + d[0]) * NY + d[1]


def nt_dot(a, b):
    return lax.dot_general(
        a, b, (((1,), (1,)), ((), ())), preferred_element_type=jnp.float32
    )


def iota(shape, axis):
    return lax.broadcasted_iota(jnp.int32, shape, axis)


def centroid_kernel(
    emb_hbm, own, slot, cnt, par2, par3, reseed, donor,
    out2, out3, out4,
    emb, sbuf, rbuf, onehot, pos, lab_send, lab_recv, lab_t, ring_q, ring_s, acc, turn, mass_two, w_send, w_recv,
    info_z, info_w, tab, req, red_z, red_w, red_c, totals, picked, donors_c,
    part, core_send, core_recv, three_q, three_s, acc3, turn3, ring_d, rows_d, send_d, recv_d, final_d,
    recv_xy, recv_three, three, recv_four, recv_out, acc_four,
    load_sem, s_sem, r_sem, q_send, q_recv, sc_send, sc_recv, once, core_s, core_r, s3_sem, r3_sem, sc3_send, sc3_recv,
    sd_sem, rd_sem,
):
    load = pltpu.make_async_copy(emb_hbm, emb, load_sem.at[0])
    load.start()
    rows, width = emb.shape
    half = width // 2
    clusters = out2.shape[0]
    per_z = out3.shape[0]
    mine = per_z // NC
    w = lax.axis_index("wide")
    z = lax.axis_index("narrow")
    x, y, c = w // 8, (w // 2) % 4, w % 2

    def wide_index(d):
        return ((x + d[0]) % NX) * 8 + ((y + d[1]) % NY) * 2 + (c + d[2]) % NC

    def wide_peer(d):
        return (wide_index(d), z)

    def offset(k):
        return (k // NY) % NX, k % NY, k // (NX * NY)

    def source_of(k):
        dx, dy, dc = offset(k)
        return wide_index((NX - dx, NY - dy, dc))

    def z_peer(k):
        return (w, (z + k) % NZ)

    barrier = pltpu.get_barrier_semaphore()
    for d in WIDE_ORDER:
        pl.semaphore_signal(barrier, inc=1, device_id=wide_peer(d), device_id_type=MESH)
    for k in range(1, NZ):
        pl.semaphore_signal(barrier, inc=1, device_id=z_peer(k), device_id_type=MESH)

    def spread(src, dst, sems, device):
        return pltpu.make_async_remote_copy(
            src_ref=src, dst_ref=dst, send_sem=sems.at[0], recv_sem=sems.at[1],
            device_id=device, device_id_type=MESH,
        )

    def spread_z(src, dst, sems):
        for k in range(1, NZ):
            spread(src, dst.at[k], sems, z_peer(k)).start()

    def join_z(dst, sems):
        at = pl.ds(1, NZ - 1)
        spread(dst.at[at], dst.at[at], sems, z_peer(1)).wait()

    def spread_xy(src, dst, sems):
        for dx, dy in XY_ORDER:
            spread(src, dst.at[dx * NY + dy], sems, wide_peer((dx, dy, 0))).start()

    def join_xy(dst, sems):
        at = pl.ds(1, NX * NY - 1)
        spread(dst.at[at], dst.at[at], sems, wide_peer((0, 1, 0))).wait()

    def to_core(dst, sems):
        here, there = pl.ds(0, NX * NY), pl.ds(NX * NY, NX * NY)
        return spread(dst.at[here], dst.at[there], sems, wide_peer((0, 0, 1)))

    sem_info_z, sem_info_w, sem_lab, sem_w = once.at[0], once.at[1], once.at[2], once.at[3]
    sem_red_z, sem_red_w, sem_xy, sem_d = once.at[4], once.at[5], once.at[6], once.at[7]
    sem_three, sem_four, sem_out = once.at[8], once.at[9], once.at[10]
    sem_info_c, sem_red_c, sem_three_c = once.at[11], once.at[12], once.at[13]
    sem_out_c, sem_donors_c = once.at[14], once.at[15]

    slots = iota((1, clusters), 1)
    parent = par2[...].astype(jnp.float32)
    hits = [slots == reseed[0:1, k : k + 1] for k in range(2)]
    grands = [jnp.sum(jnp.where(h, parent, 0.0), axis=1, keepdims=True) for h in hits]
    table = parent + jnp.where(hits[0] | hits[1], 1024.0, 0.0)
    lane = iota((1, 128), 1)
    extra = jnp.zeros((1, 128), jnp.float32)
    for i, v in enumerate(
        [donor[0:1, 0:1], donor[0:1, 1:2], grands[0], grands[1], reseed[0:1, 0:1], reseed[0:1, 1:2]]
    ):
        extra = jnp.where(lane == i, v.astype(jnp.float32), extra)
    info_z[0, :, 0:clusters] = jnp.where(iota((NZ, clusters), 0) == z, table, 0.0)
    info_z[0, :, clusters : clusters + 128] = jnp.where(iota((NZ, 128), 0) == z, extra, 0.0)

    pl.semaphore_wait(barrier, NW - 1 + NZ - 1)
    spread_z(info_z.at[0], info_z, sem_info_z)

    owner = own[...]
    target = owner // NZ
    rel = (
        ((target - c) & 1) * 16 + ((target // 8 - x) & 3) * 4 + (((target // 2) - y) & 3)
    )
    step = 256
    upper = (iota((step, step), 0) < iota((step, step), 1)).astype(jnp.bfloat16)
    carry = jnp.zeros((step, 1), jnp.float32)
    for b in range(rows // step):
        cols = slice(b * step, (b + 1) * step)
        hit = iota((step, step), 0) == owner[:, cols]
        mark = hit.astype(jnp.bfloat16)
        earlier = jnp.dot(mark, upper, preferred_element_type=jnp.float32) + carry
        mark32 = hit.astype(jnp.float32)
        rank = jnp.sum(earlier * mark32, axis=0, keepdims=True)
        carry = carry + jnp.sum(mark32, axis=1, keepdims=True)
        pos[0:1, cols] = rel[:, cols] * CAP + rank.astype(jnp.int32)
    pos[1:2, :] = owner % NZ


    places = NW * CAP
    tile = 256

    def fill_onehot(where_row):
        for i in range(places // tile):
            ids = iota((tile, rows), 0) + i * tile
            onehot[i * tile : (i + 1) * tile, :] = (ids == where_row).astype(jnp.bfloat16)

    def send_wide(src, dst, sem_s, sem_r):
        sign = 1 - 2 * c
        for d in WIDE_ORDER:
            to = ((d[0] * sign + NX) % NX, (d[1] * sign + NY) % NY, d[2])
            at = pl.ds(pl.multiple_of(rel_of(to) * CAP, CAP), CAP)
            pltpu.make_async_remote_copy(
                src_ref=src.at[at], dst_ref=dst.at[at], send_sem=sem_s, recv_sem=sem_r,
                device_id=wide_peer(to), device_id_type=MESH,
            ).start()

    def all_wide(src, dst, sem_s, sem_r):
        at = pl.ds(CAP, places - CAP)
        return pltpu.make_async_remote_copy(
            src_ref=src.at[at], dst_ref=dst.at[at], send_sem=sem_s, recv_sem=sem_r,
            device_id=wide_peer((0, 0, 1)), device_id_type=MESH,
        )


    def block_f(t):
        return (z + 2 * NZ - 1 - t) % NZ

    def block_b(t):
        return (z + 1 + t) % NZ

    def pack_half(t, h):
        b = lax.rem(t, SEND_BUFFERS)
        blk = (block_f, block_b)[h](t)
        fill_onehot(jnp.where(pos[1:2, :] == blk, pos[0:1, :], -1))

        def column(n, _):
            at = pl.ds(pl.multiple_of(h * half + n * tile, tile), tile)
            sbuf[b, :, at] = jnp.dot(
                onehot[...], emb[:, at], preferred_element_type=jnp.float32
            ).astype(jnp.bfloat16)
            return 0

        lax.fori_loop(0, half // tile, column, 0)

    def pack(t):
        b = lax.rem(t, SEND_BUFFERS)

        @pl.when(t >= SEND_BUFFERS)
        def _():
            all_wide(sbuf.at[b], rbuf.at[t], s_sem.at[b], r_sem.at[t]).wait_send()

        for h in range(2):
            pack_half(t, h)
        rbuf[t, 0:CAP, :] = sbuf[b, 0:CAP, :]

    def send(t):
        b = lax.rem(t, SEND_BUFFERS)
        send_wide(sbuf.at[b], rbuf.at[t], s_sem.at[b], r_sem.at[t])

    join_z(info_z, sem_info_z)
    whole = info_z[0]
    for k in range(1, NZ):
        whole = whole + info_z[k]
    info_w[0] = whole
    spread_xy(info_w.at[0], info_w, sem_info_w)
    load.wait()
    pack_half(0, 0)
    join_xy(info_w, sem_info_w)
    to_core(info_w, sem_info_c).start()
    pack_half(0, 1)
    rbuf[0, 0:CAP, :] = sbuf[0, 0:CAP, :]
    send(0)

    turn[...] = jnp.zeros(turn.shape, jnp.float32)
    turn3[...] = jnp.zeros(turn3.shape, jnp.float32)

    def turn_labels():
        all_wide(lab_send, lab_recv, sem_lab.at[0], sem_lab.at[1]).wait()
        eye = (iota((16, 128), 0) == iota((16, 128), 1)).astype(jnp.bfloat16)
        lab_t[...] = nt_dot(eye, lab_recv[...])

    def matched(blk):
        ids = iota((clusters, places), 0).astype(jnp.float32)
        return ids == lab_t[pl.ds(2 * blk, 1), :], lab_t[pl.ds(2 * blk + 1, 1), :]

    def weigh(k, _):
        hit, counts = matched((z + k) % NZ)
        counts = jnp.broadcast_to(counts, (8, places)).astype(jnp.bfloat16)
        w_send[k] = nt_dot(counts, hit.astype(jnp.float32).astype(jnp.bfloat16))
        return 0

    def send_masses():
        lax.fori_loop(0, NZ, weigh, 0)
        for k in range(1, NZ):
            spread(w_send.at[k], w_recv.at[k], sem_w, z_peer(k)).start()

    def join_masses():
        others = pl.ds(1, NZ - 1)
        spread(w_send.at[others], w_recv.at[others], sem_w, z_peer(1)).wait()
        total = w_send[0]
        for k in range(1, NZ):
            total = total + w_recv[k]
        diagonal = iota((clusters, clusters), 0) == iota((clusters, clusters), 1)
        mass = jnp.sum(jnp.where(diagonal, total[0:1, :], 0.0), axis=1, keepdims=True)
        mass_two[...] = jnp.broadcast_to(jnp.maximum(mass, 1.0), mass_two.shape)

    to_core(info_w, sem_info_c).wait()

    devices = NW * NZ

    def arrange(k, _):
        src = source_of(k)
        tab[pl.ds(pl.multiple_of(src * NZ, NZ), NZ), :] = info_w[k, :, 0:clusters]
        for zz in range(NZ):
            row = (src % 2) * (devices // NC) + zz * (NX * NY) + src // 2
            req[pl.ds(row, 1), :] = info_w[k, zz : zz + 1, clusters : clusters + 128]
        return 0

    lax.fori_loop(0, NW, arrange, 0)
    across = jnp.transpose(tab[...])
    high = jnp.floor(across * (1.0 / 64.0))
    low = (across - 64.0 * high).astype(jnp.bfloat16)
    high = high.astype(jnp.bfloat16)
    for b in range(rows // step):
        cols = slice(b * step, (b + 1) * step)
        mark = (iota((step, step), 0) == own[:, cols]).astype(jnp.bfloat16)
        values = 64.0 * jnp.dot(high, mark, preferred_element_type=jnp.float32) + jnp.dot(
            low, mark, preferred_element_type=jnp.float32
        )
        found = jnp.sum(
            jnp.where(iota((clusters, step), 0) == slot[:, cols], values, 0.0),
            axis=0, keepdims=True,
        ).astype(jnp.int32)
        gone = found >= 1024
        true_parent = jnp.where(gone, found - 1024, found)
        pos[2:3, cols] = jnp.where(gone, -1, true_parent)
        pos[3:4, cols] = true_parent

    place = iota((devices, 1), 0)
    owner_of = ((place % 16) * NC + place // 128) * NZ + (place // 16) % NZ
    ident = own[...] * clusters + slot[...]
    for k in range(2):
        asked = owner_of * clusters + req[:, 4 + k : 5 + k].astype(jnp.int32)
        onehot[k * devices : (k + 1) * devices, :] = (asked == ident).astype(jnp.bfloat16)
    counts32 = cnt[...].astype(jnp.float32)
    counts8 = jnp.broadcast_to(counts32, (8, rows)).astype(jnp.bfloat16)
    true_parent = pos[3:4, :]
    by_z = jnp.where(iota((8, rows), 0) == true_parent // per_z, counts32, 0.0).astype(jnp.bfloat16)
    inside = (iota((per_z, rows), 0) == true_parent % per_z).astype(jnp.bfloat16)
    asked_weights = nt_dot(counts8, onehot[...])
    folded = jnp.zeros((8, 128), jnp.float32)
    for i in range(2 * devices // 128):
        folded = jnp.where(
            iota((8, 128), 0) == i, asked_weights[:, i * 128 : (i + 1) * 128], folded
        )
    red_z[0, :, 0:128] = folded
    red_z[0, :, 128 : 128 + per_z] = nt_dot(by_z, inside)
    spread_z(red_z.at[0], red_z, sem_red_z)

    fill_onehot(pos[0:1, :])
    deep = iota((128, rows), 0)
    z_of = pos[1:2, :]
    labels = jnp.where(
        deep == 2 * z_of, slot[...], jnp.where(deep == 2 * z_of + 1, cnt[...], 0)
    ).astype(jnp.float32).astype(jnp.bfloat16)
    lab_send[...] = nt_dot(onehot[...], labels).astype(jnp.bfloat16)
    lab_recv[0:CAP, :] = lab_send[0:CAP, :]
    send_wide(lab_send, lab_recv, sem_lab.at[0], sem_lab.at[1])

    def reduce_weights_z():
        join_z(red_z, sem_red_z)
        total = red_z[0]
        for k in range(1, NZ):
            total = total + red_z[k]
        red_w[0] = total
        spread_xy(red_w.at[0], red_w, sem_red_w)

    def reduce_weights_wide():
        join_xy(red_w, sem_red_w)
        total = red_w[0].astype(jnp.int32)
        for k in range(1, NX * NY):
            total = total + red_w[k].astype(jnp.int32)
        red_c[0] = total
        swap = spread(red_c.at[0], red_c.at[1], sem_red_c, wide_peer((0, 0, 1)))
        swap.start()
        swap.wait()
        total = (total + red_c[1]).astype(jnp.float32)
        for i in range(2 * devices // 128):
            totals[0:1, i * 128 : (i + 1) * 128] = total[i : i + 1, 0:128]
        totals[:, 2 * devices : 2 * devices + per_z] = total[:, 128 : 128 + per_z]

    def pick_donors():
        first = (w * NZ + z) * rows
        for k in range(2):
            local = req[:, k : k + 1].astype(jnp.int32) - first
            onehot[k * devices : (k + 1) * devices, :] = (
                iota((devices, rows), 1) == local
            ).astype(jnp.bfloat16)

        def column(n, _):
            at = pl.ds(pl.multiple_of(n * tile, tile), tile)
            picked[:, at] = jnp.dot(
                onehot[...], emb[:, at], preferred_element_type=jnp.float32
            ).astype(jnp.bfloat16)
            return 0

        lax.fori_loop(0, width // tile, column, 0)
        for k in range(2):
            donors_copy(k).start()

    def donors_copy(k):
        at = pl.ds(pl.multiple_of(k * devices + (1 - c) * 128, 128), 128)
        return spread(picked.at[at], donors_c.at[k], sem_donors_c, wide_peer((0, 0, 1)))

    def core_copy(s):
        b = lax.rem(s, 2)
        return pltpu.make_async_remote_copy(
            src_ref=core_send.at[b], dst_ref=core_recv.at[s],
            send_sem=core_s.at[b], recv_sem=core_r.at[s],
            device_id=wide_peer((0, 0, 1)), device_id_type=MESH,
        )

    def three_terms(value):
        first = value.astype(jnp.bfloat16)
        rest = value - first.astype(jnp.float32)
        second = rest.astype(jnp.bfloat16)
        return first, second, (rest - second.astype(jnp.float32)).astype(jnp.bfloat16)

    def local_three(s):
        b = lax.rem(s, 2)

        @pl.when(s >= 2)
        def _():
            core_copy(s - 2).wait_send()

        grand_rows = jnp.transpose(req[...])
        for h, blk in enumerate((block_f(s), block_b(s))):
            base = jnp.where(
                iota((per_z, rows), 0) + per_z * blk == pos[2:3, :], cnt[...], 0
            ).astype(jnp.float32).astype(jnp.bfloat16)
            ids = (iota((per_z, devices), 0) + per_z * blk).astype(jnp.float32)
            heavy = [
                three_terms(
                    jnp.where(
                        ids == grand_rows[2 + k : 3 + k, :],
                        totals[0:1, k * devices : (k + 1) * devices],
                        0.0,
                    )
                )
                for k in range(2)
            ]
            for n in range(half // tile):
                at = slice(h * half + n * tile, h * half + (n + 1) * tile)
                value = jnp.dot(base, emb[:, at], preferred_element_type=jnp.float32)
                for k in range(2):
                    for term in heavy[k]:
                        value = value + jnp.dot(
                            term,
                            picked[k * devices : (k + 1) * devices, at],
                            preferred_element_type=jnp.float32,
                        )
                part[b, h, :, n * tile : (n + 1) * tile] = value
            core_send[b, h] = part[b, h, pl.ds(pl.multiple_of((1 - c) * mine, mine), mine), :]
        core_copy(s).start()

    groups = half // 128

    def fixed_ring(q, sc, total, turned, q_sems, sc_sems):
        rows_in, lanes = total.shape[1], turned.shape[1]

        def copies(h, t):
            to = z_peer((1, NZ - 1)[h])
            return [
                pltpu.make_async_remote_copy(
                    src_ref=ref.at[h, t], dst_ref=ref.at[h, t + 1],
                    send_sem=sems[0].at[h, t], recv_sem=sems[1].at[h, t + 1],
                    device_id=to, device_id_type=MESH,
                )
                for ref, sems in ((q, q_sems), (sc, sc_sems))
            ]

        def take_in(h, t):
            for copy in copies(h, t - 1):
                copy.wait_recv()
            turned[0:8, :] = sc[h, t]
            scale = jnp.transpose(turned[...])[0:rows_in, :] * (1.0 / TOP)
            for j in range(groups):
                at = slice(j * 128, (j + 1) * 128)
                value = q[h, t, :, at].astype(jnp.int32).astype(jnp.float32)
                total[h, :, at] += value * scale[:, j : j + 1]

        def pass_on(h, t):
            scale = jnp.zeros((rows_in, 128), jnp.float32)
            for j in range(groups):
                at = slice(j * 128, (j + 1) * 128)
                value = total[h, :, at]
                top = jnp.maximum(jnp.max(jnp.abs(value), axis=1, keepdims=True), 1e-37)
                scale = jnp.where(iota((rows_in, 128), 1) == j, top, scale)
                q[h, t, :, at] = (
                    jnp.round(value * (1.0 / top) * TOP).astype(jnp.int32).astype(jnp.int16)
                )
            if rows_in < lanes:
                filler = jnp.zeros((lanes - rows_in, 128), jnp.float32)
                scale = jnp.concatenate([scale, filler], axis=0)
            sc[h, t] = jnp.transpose(scale)[0:8, :]
            for copy in copies(h, t):
                copy.start()

        def drain(h, t):
            for copy in copies(h, t):
                copy.wait_send()

        return take_in, pass_on, drain

    take_in, pass_on, drain_two = fixed_ring(
        ring_q, ring_s, acc, turn, (q_send, q_recv), (sc_send, sc_recv)
    )
    take_three, pass_three, drain_three = fixed_ring(
        three_q, three_s, acc3, turn3, (s3_sem, r3_sem), (sc3_send, sc3_recv)
    )

    def ring_d_copy(h, s):
        return pltpu.make_async_remote_copy(
            src_ref=ring_d.at[h, s], dst_ref=ring_d.at[h, s + 1],
            send_sem=sd_sem.at[h, s], recv_sem=rd_sem.at[h, s + 1],
            device_id=z_peer((1, NZ - 1)[h]), device_id_type=MESH,
        )

    def step_three(s):
        @pl.when(s < NZ - 1)
        def _():
            local_three(s + 1)

        b = lax.rem(s, 2)
        core_copy(s).wait_recv()
        for h, blk in enumerate((block_f(s), block_b(s))):
            at = pl.ds(pl.multiple_of(c * mine, mine), mine)
            acc3[h] = part[b, h, at, :] + core_recv[s, h]
            at = pl.ds(pl.multiple_of(h * devices + c * 128 + blk * 16, 16), 16)
            chosen = (
                picked[at, :].astype(jnp.float32)
                + donors_c[h, pl.ds(pl.multiple_of(blk * 16, 16), 16), :].astype(jnp.float32)
            ).astype(jnp.bfloat16)

            @pl.when(s == 0)
            def _(h=h, chosen=chosen):
                ring_d[h, s] = chosen

            @pl.when(s > 0)
            def _(h=h, chosen=chosen):
                take_three(h, s)
                ring_d_copy(h, s - 1).wait_recv()
                ring_d[h, s] = (
                    ring_d[h, s].astype(jnp.float32) + chosen.astype(jnp.float32)
                ).astype(jnp.bfloat16)

            @pl.when(s < NZ - 1)
            def _(h=h):
                pass_three(h, s)
                ring_d_copy(h, s).start()

    quarter = width // 4

    def piece(xx, yy):
        i = xx * NY + yy
        return acc3.at[i // 8, pl.ds(pl.multiple_of((i % 8) * 8, 8), 8)]

    def send_three_and_donors():
        recv_xy[0] = piece(x, y)[...]
        for dx, dy in XY_ORDER:
            spread(
                piece((x + dx) % NX, (y + dy) % NY), recv_xy.at[dx * NY + dy], sem_xy,
                wide_peer((dx, dy, 0)),
            ).start()
        for h in range(2):
            rows_d[h] = ring_d[h, NZ - 1].astype(jnp.float32)

        def lay(k, _):
            to = wide_index(offset(k)) // NC
            for h in range(2):
                for j in range(4):
                    send_d[k, 4 * h + j : 4 * h + j + 1, :] = rows_d[
                        h, pl.ds(to, 1), j * quarter : (j + 1) * quarter
                    ]
            return 0

        lax.fori_loop(0, NX * NY, lay, 0)
        recv_d[0] = send_d[0]
        for dx, dy in XY_ORDER:
            k = dx * NY + dy
            spread(send_d.at[k], recv_d.at[k], sem_d, wide_peer((dx, dy, 0))).start()

    def join_three_and_donors():
        join_xy(recv_xy, sem_xy)
        total = recv_xy[0]
        for k in range(1, NX * NY):
            total = total + recv_xy[k]
        recv_three[0] = total
        join_xy(recv_d, sem_d)
        total = recv_d[0]
        for k in range(1, NX * NY):
            total = total + recv_d[k]
        final_d[...] = total

    def finish_three():
        join_xy(recv_three, sem_three)
        to_core(recv_three, sem_three_c).start()
        to_core(recv_three, sem_three_c).wait()

        def lay(k, _):
            src = source_of(k)
            i = src // 2
            row = (src % 2) * mine + (i % 8) * 8
            three[i // 8, pl.ds(pl.multiple_of(row, 8), 8), :] = recv_three[k]
            return 0

        lax.fori_loop(0, NW, lay, 0)
        masses = totals[:, 2 * devices : 2 * devices + per_z]
        mass_row = jnp.sum(
            jnp.where(iota((8, per_z), 0) == z, masses, 0.0), axis=0, keepdims=True
        )
        diagonal = iota((per_z, per_z), 0) == iota((per_z, per_z), 1)
        mass = jnp.sum(jnp.where(diagonal, mass_row, 0.0), axis=1, keepdims=True)
        mass = jnp.maximum(mass, 1.0)
        chosen = par3[...] == iota((8, per_z), 0) + 8 * w
        pick = chosen.astype(jnp.float32).astype(jnp.bfloat16)
        for h in range(2):
            out3[:, h * half : (h + 1) * half] = three[h] / mass
            total = jnp.zeros((8, half), jnp.float32)
            for term in three_terms(three[h]):
                total = total + jnp.dot(pick, term, preferred_element_type=jnp.float32)
            recv_four[0, :, h * half : (h + 1) * half] = total
        mass_four = jnp.sum(jnp.where(chosen, mass_row, 0.0), axis=1, keepdims=True)
        recv_four[0, :, width : width + 128] = jnp.broadcast_to(mass_four, (8, 128))
        spread_z(recv_four.at[0], recv_four, sem_four)

    def send_four():
        join_z(recv_four, sem_four)
        acc_four[...] = recv_four[z]
        for zz in range(1, NZ):
            acc_four[...] += recv_four[(z + NZ - zz) % NZ]
        mass = jnp.maximum(acc_four[:, width : width + 1], 1.0)
        recv_out[0] = acc_four[:, 0:width] / mass
        spread_xy(recv_out.at[0], recv_out, sem_out)

    def finish_four():
        to_core(recv_out, sem_out_c).wait()

        def lay(k, _):
            out4[pl.ds(pl.multiple_of(source_of(k) * 8, 8), 8), :] = recv_out[k]
            return 0

        lax.fori_loop(0, NW, lay, 0)

    def reduce_stage(t):
        all_wide(sbuf.at[0], rbuf.at[t], s_sem.at[0], r_sem.at[t]).wait_recv()
        for h, blk in enumerate((block_f(t), block_b(t))):
            hit, counts = matched(blk)
            assign = jnp.where(hit, counts, 0.0).astype(jnp.bfloat16)
            for n in range(half // tile):
                acc[h, :, n * tile : (n + 1) * tile] = jnp.dot(
                    assign,
                    rbuf[t, :, h * half + n * tile : h * half + (n + 1) * tile],
                    preferred_element_type=jnp.float32,
                )
        for h in range(2):
            pl.when(t > 0)(lambda h=h: take_in(h, t))
            pl.when(t < NZ - 1)(lambda h=h: pass_on(h, t))

    def at_stage(t, which, work):
        pl.when(t == which)(work)

    def stage(t, _):
        @pl.when(t < NZ - 1)
        def _():
            pack(t + 1)

        at_stage(t, 0, reduce_weights_z)

        @pl.when(t == 4)
        def _():
            step_three(2 * t - 1)
            send_three_and_donors()

        at_stage(t, 5, lambda: spread_xy(recv_three.at[0], recv_three, sem_three))

        @pl.when(t < NZ - 1)
        def _():
            send(t + 1)

        @pl.when(t == 0)
        def _():
            pick_donors()
            turn_labels()

        at_stage(t, 1, send_masses)

        @pl.when((t >= 1) & (t <= 3))
        def _():
            step_three(2 * t - 1)

        at_stage(t, 6, send_four)
        at_stage(t, 7, join_masses)
        reduce_stage(t)

        @pl.when(t == 0)
        def _():
            reduce_weights_wide()
            local_three(0)
            spread(donors_c, donors_c, sem_donors_c, wide_peer((0, 0, 1))).wait()

        @pl.when(t <= 3)
        def _():
            step_three(2 * t)

        at_stage(t, 4, join_three_and_donors)
        at_stage(t, 5, finish_three)
        return 0

    lax.fori_loop(0, NZ, stage, 0)

    mass = mass_two[:, 0:1]
    seeded = [iota((clusters, 1), 0) == reseed[0:1, k : k + 1] for k in range(2)]
    for j in range(4):
        at = (j % 2) * quarter
        value = acc[j // 2, :, at : at + quarter] / mass
        for k in range(2):
            value = jnp.where(seeded[k], final_d[4 * k + j : 4 * k + j + 1, :], value)
        out2[:, j * quarter : (j + 1) * quarter] = value

    join_xy(recv_out, sem_out)
    to_core(recv_out, sem_out_c).start()
    finish_four()
    for b in range(SEND_BUFFERS):
        all_wide(sbuf.at[b], rbuf.at[0], s_sem.at[b], r_sem.at[0]).wait_send()
    for b in range(2):
        core_copy(b).wait_send()

    def drain(t, _):
        for h in range(2):
            drain_two(h, t)
            drain_three(h, t)
            ring_d_copy(h, t).wait_send()
        return 0

    lax.fori_loop(0, NZ - 1, drain, 0)


def per_device(
    embeddings,
    point_counts,
    owner_ids,
    owner_slots,
    reseed_slots,
    donor_ids,
    parents_two,
    parents_three,
):
    rows, width = embeddings.shape
    clusters = parents_two.shape[0]
    per_z = parents_three.shape[0]
    half = width // 2
    places = NW * CAP
    devices = NW * NZ
    f32, bf16 = jnp.float32, jnp.bfloat16
    vmem = pl.BlockSpec(memory_space=pltpu.VMEM)
    dma = pltpu.SemaphoreType.DMA
    return pl.pallas_call(
        centroid_kernel,
        out_shape=(
            jax.ShapeDtypeStruct((clusters, width), f32),
            jax.ShapeDtypeStruct((per_z, width), f32),
            jax.ShapeDtypeStruct((L4, width), f32),
        ),
        in_specs=[pl.BlockSpec(memory_space=pl.ANY)] + [vmem] * 7,
        out_specs=(vmem,) * 3,
        scratch_shapes=[
            pltpu.VMEM((rows, width), bf16),
            pltpu.VMEM((SEND_BUFFERS, places, width), bf16),
            pltpu.VMEM((NZ, places, width), bf16),
            pltpu.VMEM((places, rows), bf16),
            pltpu.VMEM((8, rows), jnp.int32),
            pltpu.VMEM((places, 128), bf16),
            pltpu.VMEM((places, 128), bf16),
            pltpu.VMEM((16, places), f32),
            pltpu.VMEM((2, NZ, clusters, half), jnp.int16),
            pltpu.VMEM((2, NZ, 8, clusters), f32),
            pltpu.VMEM((2, clusters, half), f32),
            pltpu.VMEM((128, clusters), f32),
            pltpu.VMEM((clusters, 128), f32),
            pltpu.VMEM((NZ, 8, clusters), f32),
            pltpu.VMEM((NZ, 8, clusters), f32),
            pltpu.VMEM((NZ, NZ, clusters + 128), f32),
            pltpu.VMEM((NW, NZ, clusters + 128), f32),
            pltpu.VMEM((devices, clusters), f32),
            pltpu.VMEM((devices, 128), f32),
            pltpu.VMEM((NZ, 8, 128 + per_z), f32),
            pltpu.VMEM((NX * NY, 8, 128 + per_z), f32),
            pltpu.VMEM((2, 8, 128 + per_z), jnp.int32),
            pltpu.VMEM((8, 2 * devices + per_z), f32),
            pltpu.VMEM((2 * devices, width), bf16),
            pltpu.VMEM((2, devices // NC, width), bf16),
            pltpu.VMEM((2, 2, per_z, half), f32),
            pltpu.VMEM((2, 2, per_z // NC, half), f32),
            pltpu.VMEM((NZ, 2, per_z // NC, half), f32),
            pltpu.VMEM((2, NZ, per_z // NC, half), jnp.int16),
            pltpu.VMEM((2, NZ, 8, 128), f32),
            pltpu.VMEM((2, per_z // NC, half), f32),
            pltpu.VMEM((128, 128), f32),
            pltpu.VMEM((2, NZ, NX * NY, width), bf16),
            pltpu.VMEM((2, NX * NY, width), f32),
            pltpu.VMEM((NX * NY, 8, width // 4), f32),
            pltpu.VMEM((NX * NY, 8, width // 4), f32),
            pltpu.VMEM((8, width // 4), f32),
            pltpu.VMEM((NX * NY, 8, half), f32),
            pltpu.VMEM((NW, 8, half), f32),
            pltpu.VMEM((2, per_z, half), f32),
            pltpu.VMEM((NZ, 8, width + 128), f32),
            pltpu.VMEM((NW, 8, width), f32),
            pltpu.VMEM((8, width + 128), f32),
            dma((1,)),
            dma((SEND_BUFFERS,)),
            dma((NZ,)),
            dma((2, NZ)),
            dma((2, NZ)),
            dma((2, NZ)),
            dma((2, NZ)),
            dma((16, 2)),
            dma((2,)),
            dma((NZ,)),
            dma((2, NZ)),
            dma((2, NZ)),
            dma((2, NZ)),
            dma((2, NZ)),
            dma((2, NZ)),
            dma((2, NZ)),
        ],
        compiler_params=pltpu.CompilerParams(
            collective_id=0, has_side_effects=True, vmem_limit_bytes=63 * 2**20
        ),
    )(
        embeddings,
        owner_ids.reshape(1, rows),
        owner_slots.reshape(1, rows),
        point_counts.reshape(1, rows),
        parents_two.reshape(1, clusters),
        parents_three.reshape(1, per_z),
        reseed_slots,
        donor_ids,
    )


def solution(mesh):
    in_specs = (
        P(("wide", "narrow"), None),
        P(("wide", "narrow")),
        P(("wide", "narrow"), None),
        P(("wide", "narrow"), None),
        P(("wide", "narrow"), None),
        P(("wide", "narrow"), None),
        P(("wide", "narrow")),
        P("narrow"),
    )
    out_specs = (P(("wide", "narrow"), None), P("narrow", None), P())
    return jax.shard_map(
        per_device, mesh=mesh, in_specs=in_specs, out_specs=out_specs, check_vma=False
    )
```
